32 devices in a mesh: gx: 2 (over x), gy: 4 (over y, core), gz: 4 (over z).
Axes of the slice: x: 2, y: 2, z: 4, core: 2. Of those that a mesh axis runs over, the one named last changes fastest.
Arguments:
- state_real: float32 [4194304], P(('gx', 'gy', 'gz'))
- state_imag: float32 [4194304], P(('gx', 'gy', 'gz'))
- adjoint_real: float32 [4194304], P(('gx', 'gy', 'gz'))
- adjoint_imag: float32 [4194304], P(('gx', 'gy', 'gz'))
- energies: int32 [4194304], P(('gx', 'gy', 'gz')), may hold values from 11 to 3311, as said below
- gamma_angle: float32 [1], replicated, may hold values from 0.02 to 0.1
- beta_angle: float32 [1], replicated, may hold values from 0.1 to 0.7
Outputs:
- input_real: float32 [4194304], P(('gx', 'gy', 'gz'))
- input_imag: float32 [4194304], P(('gx', 'gy', 'gz'))
- adjoint_in_real: float32 [4194304], P(('gx', 'gy', 'gz'))
- adjoint_in_imag: float32 [4194304], P(('gx', 'gy', 'gz'))
- gamma_gradient: float32 [1], replicated
- beta_gradient: float32 [1], replicated
The draws below stay inside these ranges and needn't reach their ends.
Inputs may be any that keep to these rules, and one draw needn't show every extreme that they name: `energies`: entry j is the LABS energy sum over k from 1 to 21 of (sum over i of s_i s_(i+k))^2, with spins s_i = 1 - 2 b_i from the bits b of j XOR a mask of 22 bits drawn once.
All inputs are finite; a program needn't handle non-finite values.
Results may differ from the reference program's by a relative error of at most 0.00013.
Values sent between devices are 32-bit elements; how exact they have to be, the bound alone decides.
No kernel may reach another device: no remote copies, remote signals or barrier semaphores. Data moves between devices by JAX's collectives and lax.ppermute only.
A program may use at most 64 MiB of HBM per device.

```python
import math
import jax
import jax.numpy as jnp
from jax import lax

NQ = 22
STATE = 4194304


def count_ones_drawn(values, width):
    total = jnp.zeros_like(values)
    for bit_pos in range(width):
        total = total + (values >> bit_pos & 1)
    return total


def shared_parts(key):
    positions = jnp.arange(STATE, dtype=jnp.int32)
    subkeys = jax.random.split(key, 5)
    angles = jax.random.uniform(subkeys[0], (NQ,), jnp.float32, 0.6, 0.95)
    phases = jax.random.uniform(subkeys[1], (NQ,), jnp.float32, -0.8, 0.8)
    root_two = math.sqrt(2.0)
    prod_real = jnp.ones((STATE,), jnp.float32)
    prod_imag = jnp.zeros((STATE,), jnp.float32)
    for qubit_pos in range(NQ):
        chosen = (positions >> qubit_pos & 1).astype(jnp.float32)
        factor_real = root_two * (jnp.cos(angles[qubit_pos]) * (1.0 - chosen) + jnp.sin(angles[qubit_pos]) * jnp.cos(phases[qubit_pos]) * chosen)
        factor_imag = root_two * jnp.sin(angles[qubit_pos]) * jnp.sin(phases[qubit_pos]) * chosen
        prod_real, prod_imag = (prod_real * factor_real - prod_imag * factor_imag, prod_real * factor_imag + prod_imag * factor_real)
    noise_real = jax.random.normal(subkeys[2], (STATE,), jnp.float32)
    noise_imag = jax.random.normal(subkeys[3], (STATE,), jnp.float32)
    rising = jnp.exp(math.log(3.0) * positions.astype(jnp.float32) / STATE)
    weight = rising * jnp.exp(jax.random.uniform(subkeys[4], (STATE,), jnp.float32, 0.0, math.log(4.0)))
    return (prod_real + noise_real, prod_imag + noise_imag, weight)


def draw_state_real(key, part):
    state_part, other_part, weight = shared_parts(key)
    return state_part


def draw_state_imag(key, part):
    other_part, state_part, weight = shared_parts(key)
    return state_part


def draw_adjoint_real(key, part):
    state_part, other_part, weight = shared_parts(key)
    key = jax.random.fold_in(key, 5)
    noise = 0.7 * jax.random.normal(key, (STATE,), jnp.float32)
    return -weight * other_part / NQ + noise


def draw_adjoint_imag(key, part):
    state_part, other_part, weight = shared_parts(key)
    key = jax.random.fold_in(key, 7)
    noise = 0.7 * jax.random.normal(key, (STATE,), jnp.float32)
    return weight * state_part / NQ + noise


def draw_energies(key, part):
    key = jax.random.fold_in(key, 9)
    flip_mask = jax.random.randint(key, (), 0, 2 ** NQ, jnp.int32)
    positions = jnp.arange(STATE, dtype=jnp.int32) ^ flip_mask
    total = jnp.zeros((STATE,), jnp.int32)
    for lag_len in range(1, NQ):
        span_len = NQ - lag_len
        differ = count_ones_drawn((positions ^ positions >> lag_len) & (1 << span_len) - 1, span_len)
        correlation = span_len - 2 * differ
        total = total + correlation * correlation
    return total


def setup_inputs(seed: int = 0) -> dict:
    streams_of = jax.random.split(jax.random.key(seed), 8)
    return {
        "state_real": draw_state_real(jax.random.fold_in(streams_of[7], 71), 0),
        "state_imag": draw_state_imag(jax.random.fold_in(streams_of[7], 71), 0),
        "adjoint_real": draw_adjoint_real(jax.random.fold_in(streams_of[7], 71), 0),
        "adjoint_imag": draw_adjoint_imag(jax.random.fold_in(streams_of[7], 71), 0),
        "energies": draw_energies(jax.random.fold_in(streams_of[7], 71), 0),
        "gamma_angle": jnp.clip(jax.random.uniform(streams_of[5], (1,), jnp.float32, 0.02, 0.1), 0.02, 0.1),
        "beta_angle": jnp.clip(jax.random.uniform(streams_of[6], (1,), jnp.float32, 0.1, 0.7), 0.1, 0.7),
    }


def count_ones(values, width):
    total = jnp.zeros_like(values)
    for bit_pos in range(width):
        total = total + ((values >> bit_pos) & 1)
    return total


def hadamard(group_bits):
    indices = jnp.arange(2 ** group_bits, dtype=jnp.int32)
    parity = count_ones(indices[:, None] & indices[None, :], group_bits) & 1
    return (1 - 2 * parity).astype(jnp.float32) * jnp.float32(2.0 ** (-0.5 * group_bits))


def walsh_local(values, total_bits):
    finished = 0
    while finished < total_bits:
        group_bits = min(7, total_bits - finished)
        lower_size = 2 ** finished
        upper_size = values.shape[1] // (lower_size * 2 ** group_bits)
        matrix = hadamard(group_bits)
        if finished == 0:
            shaped = values.reshape(values.shape[0], upper_size, 2 ** group_bits)
            shaped = jnp.einsum("pak,km->pam", shaped, matrix, precision=lax.Precision.HIGHEST, preferred_element_type=jnp.float32)
        else:
            shaped = values.reshape(values.shape[0], upper_size, 2 ** group_bits, lower_size)
            shaped = jnp.einsum("pakl,km->paml", shaped, matrix, precision=lax.Precision.HIGHEST, preferred_element_type=jnp.float32)
        values = shaped.reshape(values.shape[0], -1)
        finished += group_bits
    return values


def rotate_pair(real_part, imag_part, cosine_part, sine_part):
    return real_part * cosine_part - imag_part * sine_part, real_part * sine_part + imag_part * cosine_part


def reference(state_real, state_imag, adjoint_real, adjoint_imag, energies, gamma_angle, beta_angle):
    stacked = jnp.stack([state_real, state_imag, adjoint_real, adjoint_imag])
    transformed = walsh_local(stacked, NQ)
    positions = jnp.arange(STATE, dtype=jnp.int32)
    eigenvalue = (NQ - 2 * count_ones(positions, NQ)).astype(jnp.float32)
    beta_total = jnp.sum(eigenvalue * (transformed[2] * transformed[1] - transformed[3] * transformed[0]))
    angle_beta = beta_angle[0] * eigenvalue
    cosine_part = jnp.cos(angle_beta)
    sine_part = jnp.sin(angle_beta)
    first_re, first_im = rotate_pair(transformed[0], transformed[1], cosine_part, sine_part)
    second_re, second_im = rotate_pair(transformed[2], transformed[3], cosine_part, sine_part)
    middle = walsh_local(jnp.stack([first_re, first_im, second_re, second_im]), NQ)
    energy_float = energies.astype(jnp.float32)
    gamma_total = jnp.sum(energy_float * (middle[2] * middle[1] - middle[3] * middle[0]))
    angle_gamma = gamma_angle[0] * energy_float
    cosine_cost = jnp.cos(angle_gamma)
    sine_cost = jnp.sin(angle_gamma)
    input_real, input_imag = rotate_pair(middle[0], middle[1], cosine_cost, sine_cost)
    adjoint_in_real, adjoint_in_imag = rotate_pair(middle[2], middle[3], cosine_cost, sine_cost)
    gamma_gradient = (gamma_total / STATE).reshape(1)
    beta_gradient = (beta_total / STATE).reshape(1)
    return input_real, input_imag, adjoint_in_real, adjoint_in_imag, gamma_gradient, beta_gradient
```

```python
import functools

import jax
import jax.numpy as jnp
import numpy as np
from jax import lax
from jax.experimental import pallas as pl
from jax.experimental.pallas import tpu as pltpu
from jax.sharding import PartitionSpec as P

AXES = ("gx", "gy", "gz")
LANES = 128
SUB = 8
VMEM_BYTES = 12 * 1024 * 1024
MID_VMEM_BYTES = 24 * 1024 * 1024
LARGE_VMEM_BYTES = 60 * 1024 * 1024


def sin_cos(angle):
    turns = jnp.round(angle * 0.6366197723675814)
    rest = angle - turns * 1.5703125
    rest = rest - turns * 4.837512969970703125e-4
    rest = rest - turns * 7.54978995489188216e-8
    square = rest * rest
    sine = (-1.9515295891e-4 * square + 8.3321608736e-3) * square - 1.6666654611e-1
    sine = rest + rest * square * sine
    cosine = (2.443315711809948e-5 * square - 1.388731625493765e-3) * square
    cosine = 1.0 - 0.5 * square + square * square * (cosine + 4.166664568298827e-2)
    quadrant = turns.astype(jnp.int32) & 3
    swap = (quadrant & 1) == 1
    sine, cosine = jnp.where(swap, cosine, sine), jnp.where(swap, sine, cosine)
    sine = jnp.where(quadrant >= 2, -sine, sine)
    cosine = jnp.where((quadrant == 1) | (quadrant == 2), -cosine, cosine)
    return sine, cosine


def splat(number_ref):
    return jnp.full((SUB, LANES), number_ref[0], jnp.float32)


def split_in_two(values):
    high = values.astype(jnp.bfloat16)
    return high, (values - high.astype(jnp.float32)).astype(jnp.bfloat16)


def flip_sublane(tiles, bit):
    if 2 * bit == SUB:
        return pltpu.roll(tiles, bit, 1)
    row = lax.broadcasted_iota(jnp.int32, tiles.shape, 1)
    return jnp.where(
        (row & bit) == 0, pltpu.roll(tiles, SUB - bit, 1), pltpu.roll(tiles, bit, 1)
    )


def rotate_leading(load, store, count, tangent, group_bits=3):
    finished = 0
    total = count.bit_length() - 1
    while finished < total:
        width = min(group_bits, total - finished)
        stride = 1 << finished
        size = 1 << width
        for base in range(count):
            if base & (stride * (size - 1)):
                continue
            items = [load(base + stride * pos, finished > 0) for pos in range(size)]
            for bit_pos in range(width):
                bit = 1 << bit_pos
                items = [
                    (
                        items[pos][0] - tangent * items[pos ^ bit][1],
                        items[pos][1] + tangent * items[pos ^ bit][0],
                    )
                    for pos in range(size)
                ]
            for pos in range(size):
                store(base + stride * pos, items[pos])
        finished += width


def pre_kernel(
    beta_ref, sr_ref, si_ref, ar_ref, ai_ref, out_ref, held, turned, in_sem, out_sem
):
    count, rows, _ = sr_ref.shape
    tiles = rows // SUB
    sources = (sr_ref, si_ref, ar_ref, ai_ref)

    def fetch(tile, part):
        return pltpu.make_async_copy(
            sources[part].at[:, pl.ds(tile * SUB, SUB), :],
            held.at[tile, part],
            in_sem.at[tile, part],
        )

    def write(tile, pair):
        return pltpu.make_async_copy(
            turned.at[tile, pair],
            out_ref.at[:, pl.ds(2 * pair, 2), pl.ds(tile * SUB, SUB), :],
            out_sem.at[tile, pair],
        )

    for tile in range(tiles):
        for part in range(4):
            fetch(tile, part).start()
    sine, cosine = sin_cos(splat(beta_ref))
    tangent = sine / cosine
    for tile in range(tiles):
        for pair in range(2):
            for part in range(2):
                fetch(tile, 2 * pair + part).wait()

            def load(pos, again):
                if again:
                    return turned[tile, pair, pos, 0], turned[tile, pair, pos, 1]
                return held[tile, 2 * pair, pos], held[tile, 2 * pair + 1, pos]

            def store(pos, item):
                turned[tile, pair, pos, 0] = item[0]
                turned[tile, pair, pos, 1] = item[1]

            rotate_leading(load, store, count, tangent)
            write(tile, pair).start()
    for tile in range(tiles):
        for pair in range(2):
            write(tile, pair).wait()


def pre_rotate(beta, sr, si, ar, ai):
    count, rows, _ = sr.shape
    tiles = rows // SUB
    hbm = pl.BlockSpec(memory_space=pltpu.HBM)
    size = count * rows * LANES
    return pl.pallas_call(
        pre_kernel,
        in_specs=[pl.BlockSpec(memory_space=pltpu.SMEM)] + [hbm] * 4,
        out_specs=hbm,
        out_shape=jax.ShapeDtypeStruct((count, 4, rows, LANES), jnp.float32),
        scratch_shapes=[
            pltpu.VMEM((tiles, 4, count, SUB, LANES), jnp.float32),
            pltpu.VMEM((tiles, 2, count, 2, SUB, LANES), jnp.float32),
            pltpu.SemaphoreType.DMA((tiles, 4)),
            pltpu.SemaphoreType.DMA((tiles, 2)),
        ],
        compiler_params=pltpu.CompilerParams(vmem_limit_bytes=LARGE_VMEM_BYTES),
        cost_estimate=pl.CostEstimate(
            flops=size * 40, bytes_accessed=size * 32, transcendentals=0
        ),
        name="rotate_top",
    )(beta, sr, si, ar, ai)


def prep_kernel(
    qubits, beta_ref, gamma_ref, energy_ref, matrix_ref, tangent_ref, phase_ref, found_ref
):
    sine, cosine = sin_cos(splat(beta_ref))
    tangent_ref[...] = sine / cosine
    sine, cosine = sine[:1], cosine[:1]
    scale = jnp.ones_like(cosine)
    for _ in range(qubits - 7):
        scale = scale * cosine
    powers = []
    for ones in range(8):
        value = scale
        for _ in range(7 - ones):
            value = value * cosine
        for _ in range(ones):
            value = value * sine
        powers.append(-value if ones & 2 else value)
    row = lax.broadcasted_iota(jnp.int32, (LANES, LANES), 0)
    column = lax.broadcasted_iota(jnp.int32, (LANES, LANES), 1)
    ones = lax.population_count(row ^ column)
    real_part = jnp.zeros((LANES, LANES), jnp.float32)
    imag_part = jnp.zeros((LANES, LANES), jnp.float32)
    for number in range(8):
        if number & 1:
            imag_part = jnp.where(ones == number, powers[number], imag_part)
        else:
            real_part = jnp.where(ones == number, powers[number], real_part)
    real_high, real_low = split_in_two(real_part)
    imag_high, imag_low = split_in_two(imag_part)
    for place, real_term, imag_term in (
        (0, real_high, imag_high),
        (1, real_high, imag_high),
        (2, real_low, imag_low),
    ):
        upper = pl.ds(2 * LANES * place, LANES)
        lower = pl.ds(2 * LANES * place + LANES, LANES)
        matrix_ref[upper, :LANES] = real_term
        matrix_ref[upper, LANES:] = imag_term
        matrix_ref[lower, :LANES] = -imag_term
        matrix_ref[lower, LANES:] = real_term

    local_size = energy_ref.shape[0] * LANES
    tiles = 4 * SUB
    gamma = gamma_ref[0]

    def step(pos, best):
        rows = pl.ds(pl.multiple_of(pos * tiles, tiles), tiles)
        energy = energy_ref[rows, :]
        index = (
            lax.broadcasted_iota(jnp.int32, energy.shape, 0) * LANES
            + lax.broadcasted_iota(jnp.int32, energy.shape, 1)
            + pos * (tiles * LANES)
        )
        sine_part, cosine_part = sin_cos(gamma * energy.astype(jnp.float32))
        phase_ref[0, rows, :] = cosine_part
        phase_ref[1, rows, :] = sine_part
        return jnp.maximum(best, energy * local_size + index)

    best = lax.fori_loop(
        0, energy_ref.shape[0] // tiles, step, jnp.zeros((tiles, LANES), jnp.int32)
    )
    found_ref[...] = jnp.max(best.reshape(-1, SUB, LANES), axis=0)


def prepare(qubits, beta, gamma, energies):
    rows = energies.shape[0]
    smem = pl.BlockSpec(memory_space=pltpu.SMEM)
    vmem = pl.BlockSpec(memory_space=pltpu.VMEM)
    return pl.pallas_call(
        functools.partial(prep_kernel, qubits),
        in_specs=[smem, smem, vmem],
        out_specs=[vmem] * 4,
        out_shape=[
            jax.ShapeDtypeStruct((6 * LANES, 2 * LANES), jnp.bfloat16),
            jax.ShapeDtypeStruct((SUB, LANES), jnp.float32),
            jax.ShapeDtypeStruct((2, rows, LANES), jnp.float32),
            jax.ShapeDtypeStruct((SUB, LANES), jnp.int32),
        ],
        compiler_params=pltpu.CompilerParams(vmem_limit_bytes=VMEM_BYTES),
        cost_estimate=pl.CostEstimate(
            flops=rows * LANES * 50, bytes_accessed=rows * LANES * 12, transcendentals=0
        ),
        name="phases",
    )(beta, gamma, energies)


def labs_energy(spins, qubits, count_ones):
    energy = 0
    for lag in range(1, qubits):
        span = qubits - lag
        differ = count_ones((spins ^ (spins >> lag)) & ((1 << span) - 1))
        correlation = span - 2 * differ
        energy = energy + correlation * correlation
    return energy


@functools.lru_cache(maxsize=None)
def highest_table(qubits, local_bits):
    every = 2**qubits - 1
    second = sum(2**place for place in range(0, qubits, 2))
    same = [value >> local_bits for value in (0, every, second, every ^ second)]
    low = np.arange(2**local_bits, dtype=np.int32)
    table, covered = {}, set()
    for top in range(2 ** (qubits - local_bits)):
        if top in covered:
            continue
        covered.update(top ^ value for value in same)
        energy = labs_energy(
            low | np.int32(top << local_bits),
            qubits,
            lambda bits: np.bitwise_count(bits).astype(np.int32),
        )
        highest = int(energy.max())
        places = np.flatnonzero(energy == highest)
        if highest in table or len(places) > 1:
            return None
        table[highest] = (top << local_bits) | int(places[0])
    return table


def energy_kernel(qubits, table, found_ref, out_ref):
    count, rows, _ = out_ref.shape
    block = rows * LANES
    local_bits = (count * block).bit_length() - 1
    found = found_ref[...]
    device = lax.axis_index(AXES)
    if table is None:
        mask = found
    else:
        for shift in (1, 2, 4):
            found = jnp.maximum(found, pltpu.roll(found, shift, 0))
        for shift in (1, 2, 4, 8, 16, 32, 64):
            found = jnp.maximum(found, pltpu.roll(found, shift, 1))
        highest = found >> local_bits
        mask = (found & ((1 << local_bits) - 1)) + (device << local_bits)
        for value, index in table.items():
            mask = jnp.where(highest == value, mask ^ index, mask)
    offset = (
        lax.broadcasted_iota(jnp.int32, (SUB, LANES), 0) * LANES
        + lax.broadcasted_iota(jnp.int32, (SUB, LANES), 1)
    ) ^ mask
    tiles = rows // SUB

    def step(pos, carry):
        for tile in range(tiles):
            place = (pos << local_bits) + device * block + tile * (SUB * LANES)
            spins = offset ^ place
            energy = jnp.zeros((SUB, LANES), jnp.float32)
            for lag in range(1, qubits):
                span = qubits - lag
                differ = lax.population_count((spins ^ (spins >> lag)) & ((1 << span) - 1))
                correlation = (span - 2 * differ).astype(jnp.float32)
                energy = energy + correlation * correlation
            out_ref[pos, pl.ds(tile * SUB, SUB), :] = energy
        return carry

    lax.fori_loop(0, count, step, 0)


def exchanged_energies(qubits, shape, found):
    local_bits = (shape[0] * shape[1] * shape[2]).bit_length() - 1
    table = highest_table(qubits, local_bits)
    if table is None:
        highest = sum(span * span for span in range(1, qubits))
        index = (found & ((1 << local_bits) - 1)) + (lax.axis_index(AXES) << local_bits)
        index = jnp.max(jnp.where(found >> local_bits == highest, index, -1))
        found = jnp.full((SUB, LANES), lax.pmax(index, AXES), jnp.int32)
    vmem = pl.BlockSpec(memory_space=pltpu.VMEM)
    return pl.pallas_call(
        functools.partial(energy_kernel, qubits, table),
        in_specs=[vmem],
        out_specs=vmem,
        out_shape=jax.ShapeDtypeStruct(shape, jnp.float32),
        compiler_params=pltpu.CompilerParams(vmem_limit_bytes=VMEM_BYTES),
        cost_estimate=pl.CostEstimate(
            flops=(200 << local_bits), bytes_accessed=(4 << local_bits), transcendentals=0
        ),
        name="energies",
    )(found)


def tile_place(place, number, tiles):
    first = (place * (tiles * SUB + 1) + SUB - 1) // SUB
    if number == tiles - 1 and place % SUB not in (0, SUB - 1):
        return None, (first - 1, first + tiles - 1)
    return first + number, None


def shared_tile(place, tiles):
    return ((place + 1) * (tiles * SUB + 1) - 1) // SUB


def mid_kernel(
    tangent_ref, matrix_ref, slope_ref, energy_ref, in_ref, out_ref, split, wide, edge
):
    count, rows, _ = energy_ref.shape
    tiles = rows // SUB
    tangent = tangent_ref[...]
    span = max(1, 64 // rows)

    def rows_step(pos, carry):
        some = pl.ds(pos * span, span)
        there = pl.ds(pl.multiple_of(pos * (span * rows), span * rows), span * rows)
        for pair_pos in range(2):
            pair = [
                in_ref[some, pl.ds((2 * pair_pos + part) * rows, rows), :].reshape(
                    span, tiles, SUB, LANES
                )
                for part in range(2)
            ]
            bit = 1
            while bit < tiles:
                other = [
                    jnp.concatenate(
                        [part[:, tile ^ bit : (tile ^ bit) + 1] for tile in range(tiles)], axis=1
                    )
                    for part in pair
                ]
                pair = [pair[0] - tangent * other[1], pair[1] + tangent * other[0]]
                bit *= 2
            pair = [part.reshape(span * tiles, SUB, LANES) for part in pair]
            for bit in (1, 2, 4):
                other = [flip_sublane(part, bit) for part in pair]
                pair = [pair[0] - tangent * other[1], pair[1] + tangent * other[0]]
            for part in range(2):
                first, second = split_in_two(pair[part].reshape(span * rows, LANES))
                for place, term in ((0, first), (1, second), (2, first)):
                    start = (2 * place + part) * LANES
                    split[pair_pos, there, start : start + LANES] = term
        return carry

    lax.fori_loop(0, count // span, rows_step, 0)
    half = count * rows // 2
    for pair_pos in range(2):
        for pos in range(2):
            there = pl.ds(pos * half, half)
            wide[pair_pos, there, :] = jnp.dot(
                split[pair_pos, there, :], matrix_ref[...], preferred_element_type=jnp.float32
            )

    def group(tile, bits, places):
        pairs = []
        for pair_pos in range(2):
            items = []
            for place in places:
                here = pl.ds(place * rows + tile * SUB, SUB)
                items.append([wide[pair_pos, here, :LANES], wide[pair_pos, here, LANES:]])
            for bit_pos in range(bits):
                bit = 1 << bit_pos
                items = [
                    (
                        items[pos][0] - tangent * items[pos ^ bit][1],
                        items[pos][1] + tangent * items[pos ^ bit][0],
                    )
                    for pos in range(len(places))
                ]
            pairs.append(items)
        state, adjoint = pairs
        share = 0.0
        for pos in range(len(places)):
            flipped = [
                functools.reduce(
                    jnp.add, [state[pos ^ (1 << bit)][part] for bit in range(bits)]
                )
                for part in range(2)
            ]
            share = share + (adjoint[pos][0] * flipped[1] - adjoint[pos][1] * flipped[0])
        return pairs, share

    beta_sum = slope_ref[...]
    gamma_sum = jnp.zeros((SUB, LANES), jnp.float32)
    total_bits = count.bit_length() - 1
    last_bits = min(3, total_bits)
    finished, left = last_bits, total_bits
    while finished < total_bits:
        bits = min(3, total_bits - finished)
        left -= bits
        stride = 1 << finished
        total = jnp.zeros((SUB, LANES), jnp.float32)
        for tile in range(tiles):
            for base in range(count):
                if base & (stride * ((1 << bits) - 1)):
                    continue
                places = [base + stride * pos for pos in range(1 << bits)]
                pairs, share = group(tile, bits, places)
                total = total + share
                for pair_pos, items in enumerate(pairs):
                    for place, item in zip(places, items):
                        here = pl.ds(place * rows + tile * SUB, SUB)
                        wide[pair_pos, here, :LANES] = item[0]
                        wide[pair_pos, here, LANES:] = item[1]
        for _ in range(left):
            total = total * (1.0 + tangent * tangent)
        beta_sum = beta_sum + total
        finished += bits

    block_tiles = 4 * tiles
    for base in range(0, count, 1 << last_bits):
        places = range(base, base + (1 << last_bits))
        for tile in range(tiles):
            pairs, share = group(tile, last_bits, places)
            state, adjoint = pairs
            beta_sum = beta_sum + share
            for pos, place in enumerate(places):
                value = adjoint[pos][0] * state[pos][1] - adjoint[pos][1] * state[pos][0]
                energy = energy_ref[place, pl.ds(tile * SUB, SUB), :]
                gamma_sum = gamma_sum + energy * value
                for part in range(4):
                    item = pairs[part // 2][pos][part % 2]
                    whole, halves = tile_place(place, part * tiles + tile, block_tiles)
                    if halves:
                        edge[place] = item
                    else:
                        out_ref[pl.ds(whole * SUB, SUB), :] = item

    beta_row = jnp.sum(beta_sum, axis=0, keepdims=True)
    gamma_row = jnp.sum(gamma_sum, axis=0, keepdims=True)
    half_lanes = LANES // 2
    lane = lax.broadcasted_iota(jnp.int32, (1, LANES), 1)
    value = jnp.where(
        lane < half_lanes,
        beta_row + pltpu.roll(beta_row, half_lanes, 1),
        gamma_row + pltpu.roll(gamma_row, half_lanes, 1),
    )
    value = jnp.broadcast_to(value, (SUB, LANES))
    row = lax.broadcasted_iota(jnp.int32, (SUB, LANES), 0)
    for place in range(count):
        sublane = place % SUB
        if sublane == SUB - 1:
            continue
        tile = value
        if 0 < sublane:
            tile = jnp.where(row < sublane, edge[place], tile)
        if sublane < SUB - 2:
            tile = jnp.where(row > sublane, edge[place + 1], tile)
        out_ref[pl.ds(shared_tile(place, block_tiles) * SUB, SUB), :] = tile


def mid_rotate(tangent, matrix, slope, energies, received):
    count, rows, _ = energies.shape
    size = received.size
    flat = (2, count * rows)
    out_shape = (count * (4 * rows + 1), LANES)
    vmem = pl.BlockSpec(memory_space=pltpu.VMEM)
    return pl.pallas_call(
        mid_kernel,
        in_specs=[vmem] * 5,
        out_specs=vmem,
        out_shape=jax.ShapeDtypeStruct(out_shape, jnp.float32),
        scratch_shapes=[
            pltpu.VMEM(flat + (6 * LANES,), jnp.bfloat16),
            pltpu.VMEM(flat + (2 * LANES,), jnp.float32),
            pltpu.VMEM((count, SUB, LANES), jnp.float32),
        ],
        compiler_params=pltpu.CompilerParams(vmem_limit_bytes=MID_VMEM_BYTES),
        cost_estimate=pl.CostEstimate(
            flops=size * 2 * 256 * 3, bytes_accessed=size * 8, transcendentals=0
        ),
        name="rotate_rest",
    )(tangent, matrix, slope, energies, received)


def slope_kernel(sr_ref, si_ref, ar_ref, ai_ref, out_ref):
    count, rows, _ = sr_ref.shape
    tiles = rows // SUB
    row = lax.broadcasted_iota(jnp.int32, (LANES, LANES), 0)
    column = lax.broadcasted_iota(jnp.int32, (LANES, LANES), 1)
    flips = (lax.population_count(row ^ column) == 1).astype(jnp.float32)

    def step(pos, total):
        def flipped(ref):
            own = ref[pos]
            near = own.reshape(tiles, SUB, LANES)
            result = jnp.dot(
                own,
                flips,
                precision=lax.Precision.HIGHEST,
                preferred_element_type=jnp.float32,
            ).reshape(tiles, SUB, LANES)
            for bit in (1, 2, 4):
                result = result + flip_sublane(near, bit)
            bit = 1
            while bit < tiles:
                result = result + jnp.concatenate(
                    [near[tile ^ bit : (tile ^ bit) + 1] for tile in range(tiles)], axis=0
                )
                bit *= 2
            bit = 1
            while bit < count:
                result = result + ref[pos ^ bit].reshape(tiles, SUB, LANES)
                bit *= 2
            return result

        real_part, imag_part = flipped(sr_ref), flipped(si_ref)
        adjoint_real = ar_ref[pos].reshape(tiles, SUB, LANES)
        adjoint_imag = ai_ref[pos].reshape(tiles, SUB, LANES)
        part = adjoint_real * imag_part - adjoint_imag * real_part
        return total + jnp.sum(part, axis=0)

    out_ref[...] = lax.fori_loop(0, count, step, jnp.zeros((SUB, LANES), jnp.float32))


def local_slope(sr, si, ar, ai):
    vmem = pl.BlockSpec(memory_space=pltpu.VMEM)
    return pl.pallas_call(
        slope_kernel,
        in_specs=[vmem] * 4,
        out_specs=vmem,
        out_shape=jax.ShapeDtypeStruct((SUB, LANES), jnp.float32),
        compiler_params=pltpu.CompilerParams(vmem_limit_bytes=VMEM_BYTES),
        cost_estimate=pl.CostEstimate(
            flops=sr.size * 2 * 2 * LANES * 6, bytes_accessed=sr.size * 16, transcendentals=0
        ),
        name="local_slope",
    )(sr, si, ar, ai)


def last_kernel(whole_size, phase_ref, in_ref, *refs):
    out_refs, (gamma_ref, beta_ref, done, out_sem) = refs[:4], refs[4:]
    _, count, rows, _ = phase_ref.shape
    parts = out_sem.shape[0]
    share = count // parts
    tiles = rows // SUB
    row = lax.broadcasted_iota(jnp.int32, (SUB, LANES), 0)

    def write(pos, place):
        some = pl.ds(pos * share, share)
        return pltpu.make_async_copy(
            done.at[place, some], out_refs[place].at[some], out_sem.at[pos, place]
        )

    sublane = lax.axis_index(AXES) & (SUB - 1)
    skip = (SUB - sublane) & (SUB - 1)
    below = jnp.where(sublane == SUB - 1, SUB, sublane)
    block_tiles = 4 * tiles
    block = block_tiles * SUB + 1

    def load(pos, number):
        start = pos * block
        if number < block_tiles - 1:
            return in_ref[pl.ds(start + skip + number * SUB, SUB), :]
        first = pltpu.roll(in_ref[pl.ds(start, SUB), :], sublane, 0)
        last = in_ref[pl.ds(start + block - SUB, SUB), :]
        last = pltpu.roll(last, (sublane + 1) & (SUB - 1), 0)
        whole = in_ref[pl.ds(start + block - 1 - SUB, SUB), :]
        return jnp.where(sublane == 0, whole, jnp.where(row < below, last, first))

    for part in range(parts):
        for pos in range(part * share, (part + 1) * share):
            for tile in range(tiles):
                here = pl.ds(tile * SUB, SUB)
                cosine, sine = phase_ref[0, pos, here], phase_ref[1, pos, here]
                sr, si, ar, ai = (load(pos, place * tiles + tile) for place in range(4))
                done[0, pos, here] = sr * cosine - si * sine
                done[1, pos, here] = sr * sine + si * cosine
                done[2, pos, here] = ar * cosine - ai * sine
                done[3, pos, here] = ar * sine + ai * cosine
        for place in range(4):
            write(part, place).start()
    extra = jnp.where(sublane == SUB - 1, 0, block - 1)
    total = in_ref[pl.ds(extra, 1), :]
    for pos in range(1, count):
        total = total + in_ref[pl.ds(pos * block + extra, 1), :]
    first = lax.broadcasted_iota(jnp.int32, (1, LANES), 1) < LANES // 2
    beta_ref[...] = jnp.sum(jnp.where(first, total, 0.0), axis=1, keepdims=True) / whole_size
    gamma_ref[...] = jnp.sum(jnp.where(first, 0.0, total), axis=1, keepdims=True) / whole_size
    for part in range(parts):
        for place in range(4):
            write(part, place).wait()


def last_phase(whole_size, phase, returned):
    _, count, rows, _ = phase.shape
    parts = 4
    shape = jax.ShapeDtypeStruct((count, rows, LANES), jnp.float32)
    number = jax.ShapeDtypeStruct((1, 1), jnp.float32)
    vmem = pl.BlockSpec(memory_space=pltpu.VMEM)
    hbm = pl.BlockSpec(memory_space=pltpu.HBM)
    return pl.pallas_call(
        functools.partial(last_kernel, whole_size),
        in_specs=[vmem] * 2,
        out_specs=[hbm] * 4 + [vmem] * 2,
        out_shape=[shape] * 4 + [number] * 2,
        scratch_shapes=[
            pltpu.VMEM((4, count, rows, LANES), jnp.float32),
            pltpu.SemaphoreType.DMA((parts, 4)),
        ],
        compiler_params=pltpu.CompilerParams(vmem_limit_bytes=VMEM_BYTES),
        cost_estimate=pl.CostEstimate(
            flops=returned.size * 3, bytes_accessed=returned.size * 10, transcendentals=0
        ),
        name="cost_phase",
    )(phase, returned)


def swap(values):
    return lax.all_to_all(values, AXES, split_axis=0, concat_axis=0, tiled=True)


def per_device(
    state_real, state_imag, adjoint_real, adjoint_imag, energies, gamma_angle, beta_angle
):
    local_size = state_real.shape[0]
    devices = lax.axis_size(AXES)
    whole_size = local_size * devices
    qubits = whole_size.bit_length() - 1
    shape = (devices, local_size // (devices * LANES), LANES)
    arrays = [
        part.reshape(shape) for part in (state_real, state_imag, adjoint_real, adjoint_imag)
    ]
    there = swap(pre_rotate(beta_angle, *arrays)).reshape(devices, -1, LANES)
    matrix, tangent, phase, found = prepare(
        qubits, beta_angle, gamma_angle, energies.reshape(-1, LANES)
    )
    elsewhere = exchanged_energies(qubits, shape, found)
    slope = local_slope(*arrays)
    middle = mid_rotate(tangent, matrix, slope, elsewhere, there)
    back = swap(middle.reshape(devices, -1, 1, LANES)).reshape(middle.shape)
    *outputs, gamma_gradient, beta_gradient = last_phase(
        whole_size, phase.reshape((2,) + shape), back
    )
    return tuple(part.reshape(-1) for part in outputs) + (
        gamma_gradient.reshape(1),
        beta_gradient.reshape(1),
    )


def solution(mesh):
    in_specs = (P(AXES),) * 5 + (P(), P())
    out_specs = (P(AXES),) * 4 + (P(), P())
    return jax.shard_map(
        per_device, mesh=mesh, in_specs=in_specs, out_specs=out_specs, check_vma=False
    )
```

```python
import functools

import jax
import jax.numpy as jnp
import numpy as np
from jax import lax
from jax.experimental import pallas as pl
from jax.experimental.pallas import tpu as pltpu
from jax.sharding import PartitionSpec as P

AXES = ("gx", "gy", "gz")
LANES = 128
SUB = 8
VMEM_BYTES = 12 * 1024 * 1024
MID_VMEM_BYTES = 24 * 1024 * 1024
LARGE_VMEM_BYTES = 60 * 1024 * 1024


def sin_cos(angle):
    turns = jnp.round(angle * 0.6366197723675814)
    rest = angle - turns * 1.5703125
    rest = rest - turns * 4.837512969970703125e-4
    rest = rest - turns * 7.54978995489188216e-8
    square = rest * rest
    sine = (-1.9515295891e-4 * square + 8.3321608736e-3) * square - 1.6666654611e-1
    sine = rest + rest * square * sine
    cosine = (2.443315711809948e-5 * square - 1.388731625493765e-3) * square
    cosine = 1.0 - 0.5 * square + square * square * (cosine + 4.166664568298827e-2)
    quadrant = turns.astype(jnp.int32) & 3
    swap = (quadrant & 1) == 1
    sine, cosine = jnp.where(swap, cosine, sine), jnp.where(swap, sine, cosine)
    sine = jnp.where(quadrant >= 2, -sine, sine)
    cosine = jnp.where((quadrant == 1) | (quadrant == 2), -cosine, cosine)
    return sine, cosine


def splat(number_ref):
    return jnp.full((SUB, LANES), number_ref[0], jnp.float32)


def split_in_two(values):
    high = values.astype(jnp.bfloat16)
    return high, (values - high.astype(jnp.float32)).astype(jnp.bfloat16)


def flip_sublane(tiles, bit):
    if 2 * bit == SUB:
        return pltpu.roll(tiles, bit, 1)
    row = lax.broadcasted_iota(jnp.int32, tiles.shape, 1)
    return jnp.where(
        (row & bit) == 0, pltpu.roll(tiles, SUB - bit, 1), pltpu.roll(tiles, bit, 1)
    )


def rotate_bits(items, tangent):
    bit = 1
    while bit < len(items):
        items = [
            (
                items[pos][0] - tangent * items[pos ^ bit][1],
                items[pos][1] + tangent * items[pos ^ bit][0],
            )
            for pos in range(len(items))
        ]
        bit *= 2
    return items


def pre_kernel(
    beta_ref, sr_ref, si_ref, ar_ref, ai_ref, out_ref, held, turned, in_sem, out_sem
):
    count, rows, _ = sr_ref.shape
    tiles = rows // SUB
    groups = in_sem.shape[0]
    size = count // groups
    sources = (sr_ref, si_ref, ar_ref, ai_ref)

    def fetch(group, part):
        some = pl.ds(group * size, size)
        return pltpu.make_async_copy(
            sources[part].at[some], held.at[part, some], in_sem.at[group, part]
        )

    def write(pos):
        return pltpu.make_async_copy(turned.at[pos], out_ref.at[pos], out_sem.at[pos])

    for group in range(groups):
        for part in range(4):
            fetch(group, part).start()
    sine, cosine = sin_cos(splat(beta_ref))
    tangent = sine / cosine

    def rotated(places, first, here):
        return rotate_bits(
            [(held[first, pos, here], held[first + 1, pos, here]) for pos in places], tangent
        )

    for group in range(groups):
        places = range(group * size, (group + 1) * size)
        for first in (0, 2):
            fetch(group, first).wait()
            fetch(group, first + 1).wait()
            for tile in range(tiles):
                here = pl.ds(tile * SUB, SUB)
                for pos, item in zip(places, rotated(places, first, here)):
                    held[first, pos, here] = item[0]
                    held[first + 1, pos, here] = item[1]
    for base in range(size):
        places = range(base, count, size)
        for first in (0, 2):
            for tile in range(tiles):
                here = pl.ds(tile * SUB, SUB)
                for pos, item in zip(places, rotated(places, first, here)):
                    turned[pos, first, here] = item[0]
                    turned[pos, first + 1, here] = item[1]
        for pos in places:
            write(pos).start()
    for pos in range(count):
        write(pos).wait()


def pre_rotate(beta, sr, si, ar, ai):
    count, rows, _ = sr.shape
    groups = max(1, count // 8)
    hbm = pl.BlockSpec(memory_space=pltpu.HBM)
    size = count * rows * LANES
    return pl.pallas_call(
        pre_kernel,
        in_specs=[pl.BlockSpec(memory_space=pltpu.SMEM)] + [hbm] * 4,
        out_specs=hbm,
        out_shape=jax.ShapeDtypeStruct((count, 4, rows, LANES), jnp.float32),
        scratch_shapes=[
            pltpu.VMEM((4, count, rows, LANES), jnp.float32),
            pltpu.VMEM((count, 4, rows, LANES), jnp.float32),
            pltpu.SemaphoreType.DMA((groups, 4)),
            pltpu.SemaphoreType.DMA((count,)),
        ],
        compiler_params=pltpu.CompilerParams(vmem_limit_bytes=LARGE_VMEM_BYTES),
        cost_estimate=pl.CostEstimate(
            flops=size * 40, bytes_accessed=size * 32, transcendentals=0
        ),
        name="rotate_top",
    )(beta, sr, si, ar, ai)


def prep_kernel(
    qubits, beta_ref, gamma_ref, energy_ref, matrix_ref, tangent_ref, phase_ref, found_ref
):
    sine, cosine = sin_cos(splat(beta_ref))
    tangent_ref[...] = sine / cosine
    sine, cosine = sine[:1], cosine[:1]
    scale = jnp.ones_like(cosine)
    for _ in range(qubits - 7):
        scale = scale * cosine
    powers = []
    for ones in range(8):
        value = scale
        for _ in range(7 - ones):
            value = value * cosine
        for _ in range(ones):
            value = value * sine
        powers.append(-value if ones & 2 else value)
    row = lax.broadcasted_iota(jnp.int32, (LANES, LANES), 0)
    column = lax.broadcasted_iota(jnp.int32, (LANES, LANES), 1)
    ones = lax.population_count(row ^ column)
    real_part = jnp.zeros((LANES, LANES), jnp.float32)
    imag_part = jnp.zeros((LANES, LANES), jnp.float32)
    for number in range(8):
        if number & 1:
            imag_part = jnp.where(ones == number, powers[number], imag_part)
        else:
            real_part = jnp.where(ones == number, powers[number], real_part)
    real_high, real_low = split_in_two(real_part)
    imag_high, imag_low = split_in_two(imag_part)
    for place, real_term, imag_term in (
        (0, real_high, imag_high),
        (1, real_high, imag_high),
        (2, real_low, imag_low),
    ):
        upper = pl.ds(2 * LANES * place, LANES)
        lower = pl.ds(2 * LANES * place + LANES, LANES)
        matrix_ref[upper, :LANES] = real_term
        matrix_ref[upper, LANES:] = imag_term
        matrix_ref[lower, :LANES] = -imag_term
        matrix_ref[lower, LANES:] = real_term

    local_size = energy_ref.shape[0] * LANES
    tiles = 4 * SUB
    gamma = gamma_ref[0]

    def step(pos, best):
        rows = pl.ds(pl.multiple_of(pos * tiles, tiles), tiles)
        energy = energy_ref[rows, :]
        index = (
            lax.broadcasted_iota(jnp.int32, energy.shape, 0) * LANES
            + lax.broadcasted_iota(jnp.int32, energy.shape, 1)
            + pos * (tiles * LANES)
        )
        sine_part, cosine_part = sin_cos(gamma * energy.astype(jnp.float32))
        phase_ref[0, rows, :] = cosine_part
        phase_ref[1, rows, :] = sine_part
        return jnp.maximum(best, energy * local_size + index)

    best = lax.fori_loop(
        0, energy_ref.shape[0] // tiles, step, jnp.zeros((tiles, LANES), jnp.int32)
    )
    found_ref[...] = jnp.max(best.reshape(-1, SUB, LANES), axis=0)


def prepare(qubits, beta, gamma, energies):
    rows = energies.shape[0]
    smem = pl.BlockSpec(memory_space=pltpu.SMEM)
    vmem = pl.BlockSpec(memory_space=pltpu.VMEM)
    return pl.pallas_call(
        functools.partial(prep_kernel, qubits),
        in_specs=[smem, smem, vmem],
        out_specs=[vmem] * 4,
        out_shape=[
            jax.ShapeDtypeStruct((6 * LANES, 2 * LANES), jnp.bfloat16),
            jax.ShapeDtypeStruct((SUB, LANES), jnp.float32),
            jax.ShapeDtypeStruct((2, rows, LANES), jnp.float32),
            jax.ShapeDtypeStruct((SUB, LANES), jnp.int32),
        ],
        compiler_params=pltpu.CompilerParams(vmem_limit_bytes=VMEM_BYTES),
        cost_estimate=pl.CostEstimate(
            flops=rows * LANES * 50, bytes_accessed=rows * LANES * 12, transcendentals=0
        ),
        name="phases",
    )(beta, gamma, energies)


def labs_energy(spins, qubits, count_ones):
    energy = 0
    for lag in range(1, qubits):
        span = qubits - lag
        differ = count_ones((spins ^ (spins >> lag)) & ((1 << span) - 1))
        correlation = span - 2 * differ
        energy = energy + correlation * correlation
    return energy


@functools.lru_cache(maxsize=None)
def highest_table(qubits, local_bits):
    every = 2**qubits - 1
    second = sum(2**place for place in range(0, qubits, 2))
    same = [value >> local_bits for value in (0, every, second, every ^ second)]
    low = np.arange(2**local_bits, dtype=np.int32)
    table, covered = {}, set()
    for top in range(2 ** (qubits - local_bits)):
        if top in covered:
            continue
        covered.update(top ^ value for value in same)
        energy = labs_energy(
            low | np.int32(top << local_bits),
            qubits,
            lambda bits: np.bitwise_count(bits).astype(np.int32),
        )
        highest = int(energy.max())
        places = np.flatnonzero(energy == highest)
        if highest in table or len(places) > 1:
            return None
        table[highest] = (top << local_bits) | int(places[0])
    return table


def energy_kernel(qubits, table, found_ref, out_ref):
    count, rows, _ = out_ref.shape
    block = rows * LANES
    local_bits = (count * block).bit_length() - 1
    found = found_ref[...]
    device = lax.axis_index(AXES)
    if table is None:
        mask = found
    else:
        for shift in (1, 2, 4):
            found = jnp.maximum(found, pltpu.roll(found, shift, 0))
        for shift in (1, 2, 4, 8, 16, 32, 64):
            found = jnp.maximum(found, pltpu.roll(found, shift, 1))
        highest = found >> local_bits
        mask = (found & ((1 << local_bits) - 1)) + (device << local_bits)
        for value, index in table.items():
            mask = jnp.where(highest == value, mask ^ index, mask)
    offset = (
        lax.broadcasted_iota(jnp.int32, (SUB, LANES), 0) * LANES
        + lax.broadcasted_iota(jnp.int32, (SUB, LANES), 1)
    ) ^ mask
    tiles = rows // SUB

    def step(pos, carry):
        for tile in range(tiles):
            place = (pos << local_bits) + device * block + tile * (SUB * LANES)
            spins = offset ^ place
            energy = jnp.zeros((SUB, LANES), jnp.float32)
            for lag in range(1, qubits):
                span = qubits - lag
                differ = lax.population_count((spins ^ (spins >> lag)) & ((1 << span) - 1))
                correlation = (span - 2 * differ).astype(jnp.float32)
                energy = energy + correlation * correlation
            out_ref[pos, pl.ds(tile * SUB, SUB), :] = energy
        return carry

    lax.fori_loop(0, count, step, 0)


def exchanged_energies(qubits, shape, found):
    local_bits = (shape[0] * shape[1] * shape[2]).bit_length() - 1
    table = highest_table(qubits, local_bits)
    if table is None:
        highest = sum(span * span for span in range(1, qubits))
        index = (found & ((1 << local_bits) - 1)) + (lax.axis_index(AXES) << local_bits)
        index = jnp.max(jnp.where(found >> local_bits == highest, index, -1))
        found = jnp.full((SUB, LANES), lax.pmax(index, AXES), jnp.int32)
    vmem = pl.BlockSpec(memory_space=pltpu.VMEM)
    return pl.pallas_call(
        functools.partial(energy_kernel, qubits, table),
        in_specs=[vmem],
        out_specs=vmem,
        out_shape=jax.ShapeDtypeStruct(shape, jnp.float32),
        compiler_params=pltpu.CompilerParams(vmem_limit_bytes=VMEM_BYTES),
        cost_estimate=pl.CostEstimate(
            flops=(200 << local_bits), bytes_accessed=(4 << local_bits), transcendentals=0
        ),
        name="energies",
    )(found)


def tile_place(place, number, tiles):
    first = (place * (tiles * SUB + 1) + SUB - 1) // SUB
    if number == tiles - 1 and place % SUB not in (0, SUB - 1):
        return None, (first - 1, first + tiles - 1)
    return first + number, None


def shared_tile(place, tiles):
    return ((place + 1) * (tiles * SUB + 1) - 1) // SUB


def mid_kernel(
    tangent_ref, matrix_ref, slope_ref, energy_ref, in_ref, out_ref, split, wide, edge
):
    count, rows, _ = energy_ref.shape
    tiles = rows // SUB
    tangent = tangent_ref[...]
    span = max(1, 64 // rows)

    def rotate_rows(pos, pair_pos):
        some = pl.ds(pos * span, span)
        there = pl.ds(pl.multiple_of(pos * (span * rows), span * rows), span * rows)
        pair = [
            in_ref[some, pl.ds((2 * pair_pos + part) * rows, rows), :].reshape(
                span, tiles, SUB, LANES
            )
            for part in range(2)
        ]
        bit = 1
        while bit < tiles:
            other = [
                jnp.concatenate(
                    [part[:, tile ^ bit : (tile ^ bit) + 1] for tile in range(tiles)], axis=1
                )
                for part in pair
            ]
            pair = [pair[0] - tangent * other[1], pair[1] + tangent * other[0]]
            bit *= 2
        pair = [part.reshape(span * tiles, SUB, LANES) for part in pair]
        for bit in (1, 2, 4):
            other = [flip_sublane(part, bit) for part in pair]
            pair = [pair[0] - tangent * other[1], pair[1] + tangent * other[0]]
        for part in range(2):
            first, second = split_in_two(pair[part].reshape(span * rows, LANES))
            for place, term in ((0, first), (1, second), (2, first)):
                start = (2 * place + part) * LANES
                split[pair_pos, there, start : start + LANES] = term

    def rotate_lanes(pair_pos, pos):
        there = pl.ds(pos * half, half)
        wide[pair_pos, there, :] = jnp.dot(
            split[pair_pos, there, :], matrix_ref[...], preferred_element_type=jnp.float32
        )

    half = count * rows // 2
    steps = count // span

    def two_steps(pos, carry):
        for more in range(2):
            rotate_rows(2 * pos + more, 0)
        return carry

    lax.fori_loop(0, steps // 2, two_steps, 0)
    for pos in range(2):
        rotate_lanes(0, pos)
        for step in range(pos * steps // 2, (pos + 1) * steps // 2):
            rotate_rows(step, 1)
    for pos in range(2):
        rotate_lanes(1, pos)

    def group(tile, bits, places):
        pairs = []
        for pair_pos in range(2):
            items = []
            for place in places:
                here = pl.ds(place * rows + tile * SUB, SUB)
                items.append([wide[pair_pos, here, :LANES], wide[pair_pos, here, LANES:]])
            pairs.append(rotate_bits(items, tangent))
        state, adjoint = pairs
        share = 0.0
        for pos in range(len(places)):
            flipped = [
                functools.reduce(
                    jnp.add, [state[pos ^ (1 << bit)][part] for bit in range(bits)]
                )
                for part in range(2)
            ]
            share = share + (adjoint[pos][0] * flipped[1] - adjoint[pos][1] * flipped[0])
        return pairs, share

    beta_sum = slope_ref[...]
    gamma_sum = jnp.zeros((SUB, LANES), jnp.float32)
    total_bits = count.bit_length() - 1
    last_bits = min(3, total_bits)
    finished, left = last_bits, total_bits
    while finished < total_bits:
        bits = min(3, total_bits - finished)
        left -= bits
        stride = 1 << finished
        total = jnp.zeros((SUB, LANES), jnp.float32)
        for tile in range(tiles):
            for base in range(count):
                if base & (stride * ((1 << bits) - 1)):
                    continue
                places = [base + stride * pos for pos in range(1 << bits)]
                pairs, share = group(tile, bits, places)
                total = total + share
                for pair_pos, items in enumerate(pairs):
                    for place, item in zip(places, items):
                        here = pl.ds(place * rows + tile * SUB, SUB)
                        wide[pair_pos, here, :LANES] = item[0]
                        wide[pair_pos, here, LANES:] = item[1]
        for _ in range(left):
            total = total * (1.0 + tangent * tangent)
        beta_sum = beta_sum + total
        finished += bits

    block_tiles = 4 * tiles
    for base in range(0, count, 1 << last_bits):
        places = range(base, base + (1 << last_bits))
        for tile in range(tiles):
            pairs, share = group(tile, last_bits, places)
            state, adjoint = pairs
            beta_sum = beta_sum + share
            for pos, place in enumerate(places):
                value = adjoint[pos][0] * state[pos][1] - adjoint[pos][1] * state[pos][0]
                energy = energy_ref[place, pl.ds(tile * SUB, SUB), :]
                gamma_sum = gamma_sum + energy * value
                for part in range(4):
                    item = pairs[part // 2][pos][part % 2]
                    whole, halves = tile_place(place, part * tiles + tile, block_tiles)
                    if halves:
                        edge[place] = item
                    else:
                        out_ref[pl.ds(whole * SUB, SUB), :] = item

    beta_row = jnp.sum(beta_sum, axis=0, keepdims=True)
    gamma_row = jnp.sum(gamma_sum, axis=0, keepdims=True)
    half_lanes = LANES // 2
    lane = lax.broadcasted_iota(jnp.int32, (1, LANES), 1)
    value = jnp.where(
        lane < half_lanes,
        beta_row + pltpu.roll(beta_row, half_lanes, 1),
        gamma_row + pltpu.roll(gamma_row, half_lanes, 1),
    )
    value = jnp.broadcast_to(value, (SUB, LANES))
    row = lax.broadcasted_iota(jnp.int32, (SUB, LANES), 0)
    for place in range(count):
        sublane = place % SUB
        if sublane == SUB - 1:
            continue
        tile = value
        if 0 < sublane:
            tile = jnp.where(row < sublane, edge[place], tile)
        if sublane < SUB - 2:
            tile = jnp.where(row > sublane, edge[place + 1], tile)
        out_ref[pl.ds(shared_tile(place, block_tiles) * SUB, SUB), :] = tile


def mid_rotate(tangent, matrix, slope, energies, received):
    count, rows, _ = energies.shape
    size = received.size
    flat = (2, count * rows)
    out_shape = (count * (4 * rows + 1), LANES)
    vmem = pl.BlockSpec(memory_space=pltpu.VMEM)
    return pl.pallas_call(
        mid_kernel,
        in_specs=[vmem] * 5,
        out_specs=vmem,
        out_shape=jax.ShapeDtypeStruct(out_shape, jnp.float32),
        scratch_shapes=[
            pltpu.VMEM(flat + (6 * LANES,), jnp.bfloat16),
            pltpu.VMEM(flat + (2 * LANES,), jnp.float32),
            pltpu.VMEM((count, SUB, LANES), jnp.float32),
        ],
        compiler_params=pltpu.CompilerParams(vmem_limit_bytes=MID_VMEM_BYTES),
        cost_estimate=pl.CostEstimate(
            flops=size * 2 * 256 * 3, bytes_accessed=size * 8, transcendentals=0
        ),
        name="rotate_rest",
    )(tangent, matrix, slope, energies, received)


def slope_kernel(sr_ref, si_ref, ar_ref, ai_ref, out_ref):
    count, rows, _ = sr_ref.shape
    tiles = rows // SUB
    row = lax.broadcasted_iota(jnp.int32, (LANES, LANES), 0)
    column = lax.broadcasted_iota(jnp.int32, (LANES, LANES), 1)
    flips = (lax.population_count(row ^ column) == 1).astype(jnp.float32)

    def step(pos, total):
        def flipped(ref):
            own = ref[pos]
            near = own.reshape(tiles, SUB, LANES)
            result = jnp.dot(
                own,
                flips,
                precision=lax.Precision.HIGHEST,
                preferred_element_type=jnp.float32,
            ).reshape(tiles, SUB, LANES)
            for bit in (1, 2, 4):
                result = result + flip_sublane(near, bit)
            bit = 1
            while bit < tiles:
                result = result + jnp.concatenate(
                    [near[tile ^ bit : (tile ^ bit) + 1] for tile in range(tiles)], axis=0
                )
                bit *= 2
            bit = 1
            while bit < count:
                result = result + ref[pos ^ bit].reshape(tiles, SUB, LANES)
                bit *= 2
            return result

        real_part, imag_part = flipped(sr_ref), flipped(si_ref)
        adjoint_real = ar_ref[pos].reshape(tiles, SUB, LANES)
        adjoint_imag = ai_ref[pos].reshape(tiles, SUB, LANES)
        part = adjoint_real * imag_part - adjoint_imag * real_part
        return total + jnp.sum(part, axis=0)

    out_ref[...] = lax.fori_loop(0, count, step, jnp.zeros((SUB, LANES), jnp.float32))


def local_slope(sr, si, ar, ai):
    vmem = pl.BlockSpec(memory_space=pltpu.VMEM)
    return pl.pallas_call(
        slope_kernel,
        in_specs=[vmem] * 4,
        out_specs=vmem,
        out_shape=jax.ShapeDtypeStruct((SUB, LANES), jnp.float32),
        compiler_params=pltpu.CompilerParams(vmem_limit_bytes=VMEM_BYTES),
        cost_estimate=pl.CostEstimate(
            flops=sr.size * 2 * 2 * LANES * 6, bytes_accessed=sr.size * 16, transcendentals=0
        ),
        name="local_slope",
    )(sr, si, ar, ai)


def last_kernel(whole_size, phase_ref, in_ref, *refs):
    out_refs, (gamma_ref, beta_ref, done, out_sem) = refs[:4], refs[4:]
    _, count, rows, _ = phase_ref.shape
    parts = out_sem.shape[0]
    share = count // parts
    tiles = rows // SUB
    row = lax.broadcasted_iota(jnp.int32, (SUB, LANES), 0)

    def write(pos, place):
        some = pl.ds(pos * share, share)
        return pltpu.make_async_copy(
            done.at[place, some], out_refs[place].at[some], out_sem.at[pos, place]
        )

    sublane = lax.axis_index(AXES) & (SUB - 1)
    skip = (SUB - sublane) & (SUB - 1)
    below = jnp.where(sublane == SUB - 1, SUB, sublane)
    block_tiles = 4 * tiles
    block = block_tiles * SUB + 1

    def load(pos, number):
        start = pos * block
        if number < block_tiles - 1:
            return in_ref[pl.ds(start + skip + number * SUB, SUB), :]
        first = pltpu.roll(in_ref[pl.ds(start, SUB), :], sublane, 0)
        last = in_ref[pl.ds(start + block - SUB, SUB), :]
        last = pltpu.roll(last, (sublane + 1) & (SUB - 1), 0)
        whole = in_ref[pl.ds(start + block - 1 - SUB, SUB), :]
        return jnp.where(sublane == 0, whole, jnp.where(row < below, last, first))

    for part in range(parts):
        for pos in range(part * share, (part + 1) * share):
            for tile in range(tiles):
                here = pl.ds(tile * SUB, SUB)
                cosine, sine = phase_ref[0, pos, here], phase_ref[1, pos, here]
                sr, si, ar, ai = (load(pos, place * tiles + tile) for place in range(4))
                done[0, pos, here] = sr * cosine - si * sine
                done[1, pos, here] = sr * sine + si * cosine
                done[2, pos, here] = ar * cosine - ai * sine
                done[3, pos, here] = ar * sine + ai * cosine
        for place in range(4):
            write(part, place).start()
    extra = jnp.where(sublane == SUB - 1, 0, block - 1)
    total = in_ref[pl.ds(extra, 1), :]
    for pos in range(1, count):
        total = total + in_ref[pl.ds(pos * block + extra, 1), :]
    first = lax.broadcasted_iota(jnp.int32, (1, LANES), 1) < LANES // 2
    beta_ref[...] = jnp.sum(jnp.where(first, total, 0.0), axis=1, keepdims=True) / whole_size
    gamma_ref[...] = jnp.sum(jnp.where(first, 0.0, total), axis=1, keepdims=True) / whole_size
    for part in range(parts):
        for place in range(4):
            write(part, place).wait()


def last_phase(whole_size, phase, returned):
    _, count, rows, _ = phase.shape
    parts = 8
    shape = jax.ShapeDtypeStruct((count, rows, LANES), jnp.float32)
    number = jax.ShapeDtypeStruct((1, 1), jnp.float32)
    vmem = pl.BlockSpec(memory_space=pltpu.VMEM)
    hbm = pl.BlockSpec(memory_space=pltpu.HBM)
    return pl.pallas_call(
        functools.partial(last_kernel, whole_size),
        in_specs=[vmem] * 2,
        out_specs=[hbm] * 4 + [vmem] * 2,
        out_shape=[shape] * 4 + [number] * 2,
        scratch_shapes=[
            pltpu.VMEM((4, count, rows, LANES), jnp.float32),
            pltpu.SemaphoreType.DMA((parts, 4)),
        ],
        compiler_params=pltpu.CompilerParams(vmem_limit_bytes=VMEM_BYTES),
        cost_estimate=pl.CostEstimate(
            flops=returned.size * 3, bytes_accessed=returned.size * 10, transcendentals=0
        ),
        name="cost_phase",
    )(phase, returned)


def swap(values):
    return lax.all_to_all(values, AXES, split_axis=0, concat_axis=0, tiled=True)


def per_device(
    state_real, state_imag, adjoint_real, adjoint_imag, energies, gamma_angle, beta_angle
):
    local_size = state_real.shape[0]
    devices = lax.axis_size(AXES)
    whole_size = local_size * devices
    qubits = whole_size.bit_length() - 1
    shape = (devices, local_size // (devices * LANES), LANES)
    arrays = [
        part.reshape(shape) for part in (state_real, state_imag, adjoint_real, adjoint_imag)
    ]
    there = swap(pre_rotate(beta_angle, *arrays)).reshape(devices, -1, LANES)
    matrix, tangent, phase, found = prepare(
        qubits, beta_angle, gamma_angle, energies.reshape(-1, LANES)
    )
    elsewhere = exchanged_energies(qubits, shape, found)
    slope = local_slope(*arrays)
    middle = mid_rotate(tangent, matrix, slope, elsewhere, there)
    back = swap(middle.reshape(devices, -1, 1, LANES)).reshape(middle.shape)
    *outputs, gamma_gradient, beta_gradient = last_phase(
        whole_size, phase.reshape((2,) + shape), back
    )
    return tuple(part.reshape(-1) for part in outputs) + (
        gamma_gradient.reshape(1),
        beta_gradient.reshape(1),
    )


def solution(mesh):
    in_specs = (P(AXES),) * 5 + (P(), P())
    out_specs = (P(AXES),) * 4 + (P(), P())
    return jax.shard_map(
        per_device, mesh=mesh, in_specs=in_specs, out_specs=out_specs, check_vma=False
    )
```

```python
import functools

import jax
import jax.numpy as jnp
import numpy as np
from jax import lax
from jax.experimental import pallas as pl
from jax.experimental.pallas import tpu as pltpu
from jax.sharding import PartitionSpec as P

AXES = ("gx", "gy", "gz")
SWAP_AXES = ("gy", "gx", "gz")
LANES = 128
SUB = 8
VMEM_BYTES = 12 * 1024 * 1024
MID_VMEM_BYTES = 24 * 1024 * 1024
LARGE_VMEM_BYTES = 60 * 1024 * 1024


def sin_cos(angle):
    turns = jnp.round(angle * 0.6366197723675814)
    rest = angle - turns * 1.5703125
    rest = rest - turns * 4.837512969970703125e-4
    rest = rest - turns * 7.54978995489188216e-8
    square = rest * rest
    sine = (-1.9515295891e-4 * square + 8.3321608736e-3) * square - 1.6666654611e-1
    sine = rest + rest * square * sine
    cosine = (2.443315711809948e-5 * square - 1.388731625493765e-3) * square
    cosine = 1.0 - 0.5 * square + square * square * (cosine + 4.166664568298827e-2)
    quadrant = turns.astype(jnp.int32) & 3
    swap = (quadrant & 1) == 1
    sine, cosine = jnp.where(swap, cosine, sine), jnp.where(swap, sine, cosine)
    sine = jnp.where(quadrant >= 2, -sine, sine)
    cosine = jnp.where((quadrant == 1) | (quadrant == 2), -cosine, cosine)
    return sine, cosine


def splat(number_ref):
    return jnp.full((SUB, LANES), number_ref[0], jnp.float32)


def split_in_two(values):
    high = values.astype(jnp.bfloat16)
    return high, (values - high.astype(jnp.float32)).astype(jnp.bfloat16)


def flip_sublane(tiles, bit):
    if 2 * bit == SUB:
        return pltpu.roll(tiles, bit, 1)
    row = lax.broadcasted_iota(jnp.int32, tiles.shape, 1)
    return jnp.where(
        (row & bit) == 0, pltpu.roll(tiles, SUB - bit, 1), pltpu.roll(tiles, bit, 1)
    )


def rotate_bits(items, tangent):
    bit = 1
    while bit < len(items):
        items = [
            (
                items[pos][0] - tangent * items[pos ^ bit][1],
                items[pos][1] + tangent * items[pos ^ bit][0],
            )
            for pos in range(len(items))
        ]
        bit *= 2
    return items


def rotate_leading(load, store, count, tangent, group_bits=3):
    finished = 0
    total = count.bit_length() - 1
    while finished < total:
        width = min(group_bits, total - finished)
        stride = 1 << finished
        size = 1 << width
        for base in range(count):
            if base & (stride * (size - 1)):
                continue
            items = [load(base + stride * pos, finished > 0) for pos in range(size)]
            items = rotate_bits(items, tangent)
            for pos in range(size):
                store(base + stride * pos, items[pos])
        finished += width


def pre_kernel(
    beta_ref, sr_ref, si_ref, ar_ref, ai_ref, out_ref, held, turned, in_sem, out_sem
):
    count, rows, _ = sr_ref.shape
    tiles = rows // SUB
    sources = (sr_ref, si_ref, ar_ref, ai_ref)

    def fetch(tile, part):
        return pltpu.make_async_copy(
            sources[part].at[:, pl.ds(tile * SUB, SUB), :],
            held.at[tile, part],
            in_sem.at[tile, part],
        )

    def write(tile, pair):
        return pltpu.make_async_copy(
            turned.at[tile, pair],
            out_ref.at[:, pl.ds(2 * pair, 2), pl.ds(tile * SUB, SUB), :],
            out_sem.at[tile, pair],
        )

    for tile in range(tiles):
        for part in range(4):
            fetch(tile, part).start()
    sine, cosine = sin_cos(splat(beta_ref))
    tangent = sine / cosine
    for tile in range(tiles):
        for pair in range(2):
            for part in range(2):
                fetch(tile, 2 * pair + part).wait()

            def load(pos, again):
                if again:
                    return turned[tile, pair, pos, 0], turned[tile, pair, pos, 1]
                return held[tile, 2 * pair, pos], held[tile, 2 * pair + 1, pos]

            def store(pos, item):
                turned[tile, pair, pos, 0] = item[0]
                turned[tile, pair, pos, 1] = item[1]

            rotate_leading(load, store, count, tangent)
            write(tile, pair).start()
    for tile in range(tiles):
        for pair in range(2):
            write(tile, pair).wait()


def pre_rotate(beta, sr, si, ar, ai):
    count, rows, _ = sr.shape
    tiles = rows // SUB
    hbm = pl.BlockSpec(memory_space=pltpu.HBM)
    size = count * rows * LANES
    return pl.pallas_call(
        pre_kernel,
        in_specs=[pl.BlockSpec(memory_space=pltpu.SMEM)] + [hbm] * 4,
        out_specs=hbm,
        out_shape=jax.ShapeDtypeStruct((count, 4, rows, LANES), jnp.float32),
        scratch_shapes=[
            pltpu.VMEM((tiles, 4, count, SUB, LANES), jnp.float32),
            pltpu.VMEM((tiles, 2, count, 2, SUB, LANES), jnp.float32),
            pltpu.SemaphoreType.DMA((tiles, 4)),
            pltpu.SemaphoreType.DMA((tiles, 2)),
        ],
        compiler_params=pltpu.CompilerParams(vmem_limit_bytes=LARGE_VMEM_BYTES),
        cost_estimate=pl.CostEstimate(
            flops=size * 40, bytes_accessed=size * 32, transcendentals=0
        ),
        name="rotate_top",
    )(beta, sr, si, ar, ai)


def prep_kernel(
    qubits, beta_ref, gamma_ref, energy_ref, matrix_ref, tangent_ref, phase_ref, found_ref
):
    sine, cosine = sin_cos(splat(beta_ref))
    tangent_ref[...] = sine / cosine
    sine, cosine = sine[:1], cosine[:1]
    scale = jnp.ones_like(cosine)
    for _ in range(qubits - 7):
        scale = scale * cosine
    powers = []
    for ones in range(8):
        value = scale
        for _ in range(7 - ones):
            value = value * cosine
        for _ in range(ones):
            value = value * sine
        powers.append(-value if ones & 2 else value)
    row = lax.broadcasted_iota(jnp.int32, (LANES, LANES), 0)
    column = lax.broadcasted_iota(jnp.int32, (LANES, LANES), 1)
    ones = lax.population_count(row ^ column)
    real_part = jnp.zeros((LANES, LANES), jnp.float32)
    imag_part = jnp.zeros((LANES, LANES), jnp.float32)
    for number in range(8):
        if number & 1:
            imag_part = jnp.where(ones == number, powers[number], imag_part)
        else:
            real_part = jnp.where(ones == number, powers[number], real_part)
    real_high, real_low = split_in_two(real_part)
    imag_high, imag_low = split_in_two(imag_part)
    for place, real_term, imag_term in (
        (0, real_high, imag_high),
        (1, real_high, imag_high),
        (2, real_low, imag_low),
    ):
        upper = pl.ds(2 * LANES * place, LANES)
        lower = pl.ds(2 * LANES * place + LANES, LANES)
        matrix_ref[upper, :LANES] = real_term
        matrix_ref[upper, LANES:] = imag_term
        matrix_ref[lower, :LANES] = -imag_term
        matrix_ref[lower, LANES:] = real_term

    local_size = energy_ref.shape[0] * LANES
    tiles = 4 * SUB
    gamma = gamma_ref[0]

    def step(pos, best):
        rows = pl.ds(pl.multiple_of(pos * tiles, tiles), tiles)
        energy = energy_ref[rows, :]
        index = (
            lax.broadcasted_iota(jnp.int32, energy.shape, 0) * LANES
            + lax.broadcasted_iota(jnp.int32, energy.shape, 1)
            + pos * (tiles * LANES)
        )
        sine_part, cosine_part = sin_cos(gamma * energy.astype(jnp.float32))
        phase_ref[0, rows, :] = cosine_part
        phase_ref[1, rows, :] = sine_part
        return jnp.maximum(best, energy * local_size + index)

    best = lax.fori_loop(
        0, energy_ref.shape[0] // tiles, step, jnp.zeros((tiles, LANES), jnp.int32)
    )
    found_ref[...] = jnp.max(best.reshape(-1, SUB, LANES), axis=0)


def prepare(qubits, beta, gamma, energies):
    rows = energies.shape[0]
    smem = pl.BlockSpec(memory_space=pltpu.SMEM)
    vmem = pl.BlockSpec(memory_space=pltpu.VMEM)
    return pl.pallas_call(
        functools.partial(prep_kernel, qubits),
        in_specs=[smem, smem, vmem],
        out_specs=[vmem] * 4,
        out_shape=[
            jax.ShapeDtypeStruct((6 * LANES, 2 * LANES), jnp.bfloat16),
            jax.ShapeDtypeStruct((SUB, LANES), jnp.float32),
            jax.ShapeDtypeStruct((2, rows, LANES), jnp.float32),
            jax.ShapeDtypeStruct((SUB, LANES), jnp.int32),
        ],
        compiler_params=pltpu.CompilerParams(vmem_limit_bytes=VMEM_BYTES),
        cost_estimate=pl.CostEstimate(
            flops=rows * LANES * 50, bytes_accessed=rows * LANES * 12, transcendentals=0
        ),
        name="phases",
    )(beta, gamma, energies)


def labs_energy(spins, qubits, count_ones):
    energy = 0
    for lag in range(1, qubits):
        span = qubits - lag
        differ = count_ones((spins ^ (spins >> lag)) & ((1 << span) - 1))
        correlation = span - 2 * differ
        energy = energy + correlation * correlation
    return energy


@functools.lru_cache(maxsize=None)
def highest_table(qubits, local_bits):
    every = 2**qubits - 1
    second = sum(2**place for place in range(0, qubits, 2))
    same = [value >> local_bits for value in (0, every, second, every ^ second)]
    low = np.arange(2**local_bits, dtype=np.int32)
    table, covered = {}, set()
    for top in range(2 ** (qubits - local_bits)):
        if top in covered:
            continue
        covered.update(top ^ value for value in same)
        energy = labs_energy(
            low | np.int32(top << local_bits),
            qubits,
            lambda bits: np.bitwise_count(bits).astype(np.int32),
        )
        highest = int(energy.max())
        places = np.flatnonzero(energy == highest)
        if highest in table or len(places) > 1:
            return None
        table[highest] = (top << local_bits) | int(places[0])
    return table


def energy_kernel(qubits, table, found_ref, out_ref):
    count, rows, _ = out_ref.shape
    block = rows * LANES
    local_bits = (count * block).bit_length() - 1
    found = found_ref[...]
    device = lax.axis_index(AXES)
    if table is None:
        mask = found
    else:
        for shift in (1, 2, 4):
            found = jnp.maximum(found, pltpu.roll(found, shift, 0))
        for shift in (1, 2, 4, 8, 16, 32, 64):
            found = jnp.maximum(found, pltpu.roll(found, shift, 1))
        highest = found >> local_bits
        mask = (found & ((1 << local_bits) - 1)) + (device << local_bits)
        for value, index in table.items():
            mask = jnp.where(highest == value, mask ^ index, mask)
    offset = (
        lax.broadcasted_iota(jnp.int32, (SUB, LANES), 0) * LANES
        + lax.broadcasted_iota(jnp.int32, (SUB, LANES), 1)
    ) ^ mask
    tiles = rows // SUB
    here = lax.axis_index(SWAP_AXES)

    def device_at(pos):
        places = {}
        for name in reversed(SWAP_AXES):
            width = lax.axis_size(name).bit_length() - 1
            places[name] = pos & ((1 << width) - 1)
            pos = pos >> width
        index = 0
        for name in AXES:
            index = (index << (lax.axis_size(name).bit_length() - 1)) | places[name]
        return index

    def step(pos, carry):
        for tile in range(tiles):
            place = (device_at(pos) << local_bits) + here * block + tile * (SUB * LANES)
            spins = offset ^ place
            energy = jnp.zeros((SUB, LANES), jnp.float32)
            for lag in range(1, qubits):
                span = qubits - lag
                differ = lax.population_count((spins ^ (spins >> lag)) & ((1 << span) - 1))
                correlation = (span - 2 * differ).astype(jnp.float32)
                energy = energy + correlation * correlation
            out_ref[pos, pl.ds(tile * SUB, SUB), :] = energy
        return carry

    lax.fori_loop(0, count, step, 0)


def exchanged_energies(qubits, shape, found):
    local_bits = (shape[0] * shape[1] * shape[2]).bit_length() - 1
    table = highest_table(qubits, local_bits)
    if table is None:
        highest = sum(span * span for span in range(1, qubits))
        index = (found & ((1 << local_bits) - 1)) + (lax.axis_index(AXES) << local_bits)
        index = jnp.max(jnp.where(found >> local_bits == highest, index, -1))
        found = jnp.full((SUB, LANES), lax.pmax(index, AXES), jnp.int32)
    vmem = pl.BlockSpec(memory_space=pltpu.VMEM)
    return pl.pallas_call(
        functools.partial(energy_kernel, qubits, table),
        in_specs=[vmem],
        out_specs=vmem,
        out_shape=jax.ShapeDtypeStruct(shape, jnp.float32),
        compiler_params=pltpu.CompilerParams(vmem_limit_bytes=VMEM_BYTES),
        cost_estimate=pl.CostEstimate(
            flops=(200 << local_bits), bytes_accessed=(4 << local_bits), transcendentals=0
        ),
        name="energies",
    )(found)


def tile_place(place, number, tiles):
    first = (place * (tiles * SUB + 1) + SUB - 1) // SUB
    if number == tiles - 1 and place % SUB not in (0, SUB - 1):
        return None, (first - 1, first + tiles - 1)
    return first + number, None


def shared_tile(place, tiles):
    return ((place + 1) * (tiles * SUB + 1) - 1) // SUB


def mid_kernel(
    tangent_ref, matrix_ref, slope_ref, energy_ref, in_ref, out_ref, split, wide, edge
):
    count, rows, _ = energy_ref.shape
    tiles = rows // SUB
    tangent = tangent_ref[...]
    span = max(1, 64 // rows)

    def rotate_rows(pos, pair_pos):
        some = pl.ds(pos * span, span)
        there = pl.ds(pl.multiple_of(pos * (span * rows), span * rows), span * rows)
        pair = [
            in_ref[some, pl.ds((2 * pair_pos + part) * rows, rows), :].reshape(
                span, tiles, SUB, LANES
            )
            for part in range(2)
        ]
        bit = 1
        while bit < tiles:
            other = [
                jnp.concatenate(
                    [part[:, tile ^ bit : (tile ^ bit) + 1] for tile in range(tiles)], axis=1
                )
                for part in pair
            ]
            pair = [pair[0] - tangent * other[1], pair[1] + tangent * other[0]]
            bit *= 2
        pair = [part.reshape(span * tiles, SUB, LANES) for part in pair]
        for bit in (1, 2, 4):
            other = [flip_sublane(part, bit) for part in pair]
            pair = [pair[0] - tangent * other[1], pair[1] + tangent * other[0]]
        for part in range(2):
            first, second = split_in_two(pair[part].reshape(span * rows, LANES))
            for place, term in ((0, first), (1, second), (2, first)):
                start = (2 * place + part) * LANES
                split[pair_pos, there, start : start + LANES] = term

    def rotate_lanes(pair_pos, pos):
        there = pl.ds(pos * half, half)
        wide[pair_pos, there, :] = jnp.dot(
            split[pair_pos, there, :], matrix_ref[...], preferred_element_type=jnp.float32
        )

    half = count * rows // 2
    steps = count // span

    def two_steps(pos, carry):
        for more in range(2):
            rotate_rows(2 * pos + more, 0)
        return carry

    lax.fori_loop(0, steps // 2, two_steps, 0)
    for pos in range(2):
        rotate_lanes(0, pos)
        for step in range(pos * steps // 2, (pos + 1) * steps // 2):
            rotate_rows(step, 1)
    for pos in range(2):
        rotate_lanes(1, pos)

    def group(tile, bits, places):
        pairs = []
        for pair_pos in range(2):
            items = []
            for place in places:
                here = pl.ds(place * rows + tile * SUB, SUB)
                items.append([wide[pair_pos, here, :LANES], wide[pair_pos, here, LANES:]])
            pairs.append(rotate_bits(items, tangent))
        state, adjoint = pairs
        share = 0.0
        for pos in range(len(places)):
            flipped = [
                functools.reduce(
                    jnp.add, [state[pos ^ (1 << bit)][part] for bit in range(bits)]
                )
                for part in range(2)
            ]
            share = share + (adjoint[pos][0] * flipped[1] - adjoint[pos][1] * flipped[0])
        return pairs, share

    beta_sum = slope_ref[...]
    gamma_sum = jnp.zeros((SUB, LANES), jnp.float32)
    total_bits = count.bit_length() - 1
    last_bits = min(3, total_bits)
    finished, left = last_bits, total_bits
    while finished < total_bits:
        bits = min(3, total_bits - finished)
        left -= bits
        stride = 1 << finished
        total = jnp.zeros((SUB, LANES), jnp.float32)
        for tile in range(tiles):
            for base in range(count):
                if base & (stride * ((1 << bits) - 1)):
                    continue
                places = [base + stride * pos for pos in range(1 << bits)]
                pairs, share = group(tile, bits, places)
                total = total + share
                for pair_pos, items in enumerate(pairs):
                    for place, item in zip(places, items):
                        here = pl.ds(place * rows + tile * SUB, SUB)
                        wide[pair_pos, here, :LANES] = item[0]
                        wide[pair_pos, here, LANES:] = item[1]
        for _ in range(left):
            total = total * (1.0 + tangent * tangent)
        beta_sum = beta_sum + total
        finished += bits

    block_tiles = 4 * tiles
    for base in range(0, count, 1 << last_bits):
        places = range(base, base + (1 << last_bits))
        for tile in range(tiles):
            pairs, share = group(tile, last_bits, places)
            state, adjoint = pairs
            beta_sum = beta_sum + share
            for pos, place in enumerate(places):
                value = adjoint[pos][0] * state[pos][1] - adjoint[pos][1] * state[pos][0]
                energy = energy_ref[place, pl.ds(tile * SUB, SUB), :]
                gamma_sum = gamma_sum + energy * value
                for part in range(4):
                    item = pairs[part // 2][pos][part % 2]
                    whole, halves = tile_place(place, part * tiles + tile, block_tiles)
                    if halves:
                        edge[place] = item
                    else:
                        out_ref[pl.ds(whole * SUB, SUB), :] = item

    beta_row = jnp.sum(beta_sum, axis=0, keepdims=True)
    gamma_row = jnp.sum(gamma_sum, axis=0, keepdims=True)
    half_lanes = LANES // 2
    lane = lax.broadcasted_iota(jnp.int32, (1, LANES), 1)
    value = jnp.where(
        lane < half_lanes,
        beta_row + pltpu.roll(beta_row, half_lanes, 1),
        gamma_row + pltpu.roll(gamma_row, half_lanes, 1),
    )
    value = jnp.broadcast_to(value, (SUB, LANES))
    row = lax.broadcasted_iota(jnp.int32, (SUB, LANES), 0)
    for place in range(count):
        sublane = place % SUB
        if sublane == SUB - 1:
            continue
        tile = value
        if 0 < sublane:
            tile = jnp.where(row < sublane, edge[place], tile)
        if sublane < SUB - 2:
            tile = jnp.where(row > sublane, edge[place + 1], tile)
        out_ref[pl.ds(shared_tile(place, block_tiles) * SUB, SUB), :] = tile


def mid_rotate(tangent, matrix, slope, energies, received):
    count, rows, _ = energies.shape
    size = received.size
    flat = (2, count * rows)
    out_shape = (count * (4 * rows + 1), LANES)
    vmem = pl.BlockSpec(memory_space=pltpu.VMEM)
    return pl.pallas_call(
        mid_kernel,
        in_specs=[vmem] * 5,
        out_specs=vmem,
        out_shape=jax.ShapeDtypeStruct(out_shape, jnp.float32),
        scratch_shapes=[
            pltpu.VMEM(flat + (6 * LANES,), jnp.bfloat16),
            pltpu.VMEM(flat + (2 * LANES,), jnp.float32),
            pltpu.VMEM((count, SUB, LANES), jnp.float32),
        ],
        compiler_params=pltpu.CompilerParams(vmem_limit_bytes=MID_VMEM_BYTES),
        cost_estimate=pl.CostEstimate(
            flops=size * 2 * 256 * 3, bytes_accessed=size * 8, transcendentals=0
        ),
        name="rotate_rest",
    )(tangent, matrix, slope, energies, received)


def slope_kernel(sr_ref, si_ref, ar_ref, ai_ref, out_ref):
    count, rows, _ = sr_ref.shape
    tiles = rows // SUB
    row = lax.broadcasted_iota(jnp.int32, (LANES, LANES), 0)
    column = lax.broadcasted_iota(jnp.int32, (LANES, LANES), 1)
    flips = (lax.population_count(row ^ column) == 1).astype(jnp.float32)

    def step(pos, total):
        def flipped(ref):
            own = ref[pos]
            near = own.reshape(tiles, SUB, LANES)
            result = jnp.dot(
                own,
                flips,
                precision=lax.Precision.HIGHEST,
                preferred_element_type=jnp.float32,
            ).reshape(tiles, SUB, LANES)
            for bit in (1, 2, 4):
                result = result + flip_sublane(near, bit)
            bit = 1
            while bit < tiles:
                result = result + jnp.concatenate(
                    [near[tile ^ bit : (tile ^ bit) + 1] for tile in range(tiles)], axis=0
                )
                bit *= 2
            bit = 1
            while bit < count:
                result = result + ref[pos ^ bit].reshape(tiles, SUB, LANES)
                bit *= 2
            return result

        real_part, imag_part = flipped(sr_ref), flipped(si_ref)
        adjoint_real = ar_ref[pos].reshape(tiles, SUB, LANES)
        adjoint_imag = ai_ref[pos].reshape(tiles, SUB, LANES)
        part = adjoint_real * imag_part - adjoint_imag * real_part
        return total + jnp.sum(part, axis=0)

    out_ref[...] = lax.fori_loop(0, count, step, jnp.zeros((SUB, LANES), jnp.float32))


def local_slope(sr, si, ar, ai):
    vmem = pl.BlockSpec(memory_space=pltpu.VMEM)
    return pl.pallas_call(
        slope_kernel,
        in_specs=[vmem] * 4,
        out_specs=vmem,
        out_shape=jax.ShapeDtypeStruct((SUB, LANES), jnp.float32),
        compiler_params=pltpu.CompilerParams(vmem_limit_bytes=VMEM_BYTES),
        cost_estimate=pl.CostEstimate(
            flops=sr.size * 2 * 2 * LANES * 6, bytes_accessed=sr.size * 16, transcendentals=0
        ),
        name="local_slope",
    )(sr, si, ar, ai)


def last_kernel(whole_size, phase_ref, in_ref, *refs):
    out_refs, (gamma_ref, beta_ref, done, out_sem) = refs[:4], refs[4:]
    _, count, rows, _ = phase_ref.shape
    parts = out_sem.shape[0]
    share = count // parts
    tiles = rows // SUB
    row = lax.broadcasted_iota(jnp.int32, (SUB, LANES), 0)

    def write(pos, place):
        some = pl.ds(pos * share, share)
        return pltpu.make_async_copy(
            done.at[place, some], out_refs[place].at[some], out_sem.at[pos, place]
        )

    sublane = lax.axis_index(SWAP_AXES) & (SUB - 1)
    skip = (SUB - sublane) & (SUB - 1)
    below = jnp.where(sublane == SUB - 1, SUB, sublane)
    block_tiles = 4 * tiles
    block = block_tiles * SUB + 1

    def load(pos, number):
        start = pos * block
        if number < block_tiles - 1:
            return in_ref[pl.ds(start + skip + number * SUB, SUB), :]
        first = pltpu.roll(in_ref[pl.ds(start, SUB), :], sublane, 0)
        last = in_ref[pl.ds(start + block - SUB, SUB), :]
        last = pltpu.roll(last, (sublane + 1) & (SUB - 1), 0)
        whole = in_ref[pl.ds(start + block - 1 - SUB, SUB), :]
        return jnp.where(sublane == 0, whole, jnp.where(row < below, last, first))

    for part in range(parts):
        for pos in range(part * share, (part + 1) * share):
            for tile in range(tiles):
                here = pl.ds(tile * SUB, SUB)
                cosine, sine = phase_ref[0, pos, here], phase_ref[1, pos, here]
                sr, si, ar, ai = (load(pos, place * tiles + tile) for place in range(4))
                done[0, pos, here] = sr * cosine - si * sine
                done[1, pos, here] = sr * sine + si * cosine
                done[2, pos, here] = ar * cosine - ai * sine
                done[3, pos, here] = ar * sine + ai * cosine
        for place in range(4):
            write(part, place).start()
    extra = jnp.where(sublane == SUB - 1, 0, block - 1)
    total = in_ref[pl.ds(extra, 1), :]
    for pos in range(1, count):
        total = total + in_ref[pl.ds(pos * block + extra, 1), :]
    first = lax.broadcasted_iota(jnp.int32, (1, LANES), 1) < LANES // 2
    beta_ref[...] = jnp.sum(jnp.where(first, total, 0.0), axis=1, keepdims=True) / whole_size
    gamma_ref[...] = jnp.sum(jnp.where(first, 0.0, total), axis=1, keepdims=True) / whole_size
    for part in range(parts):
        for place in range(4):
            write(part, place).wait()


def last_phase(whole_size, phase, returned):
    _, count, rows, _ = phase.shape
    parts = 4
    shape = jax.ShapeDtypeStruct((count, rows, LANES), jnp.float32)
    number = jax.ShapeDtypeStruct((1, 1), jnp.float32)
    vmem = pl.BlockSpec(memory_space=pltpu.VMEM)
    hbm = pl.BlockSpec(memory_space=pltpu.HBM)
    return pl.pallas_call(
        functools.partial(last_kernel, whole_size),
        in_specs=[vmem] * 2,
        out_specs=[hbm] * 4 + [vmem] * 2,
        out_shape=[shape] * 4 + [number] * 2,
        scratch_shapes=[
            pltpu.VMEM((4, count, rows, LANES), jnp.float32),
            pltpu.SemaphoreType.DMA((parts, 4)),
        ],
        compiler_params=pltpu.CompilerParams(vmem_limit_bytes=VMEM_BYTES),
        cost_estimate=pl.CostEstimate(
            flops=returned.size * 3, bytes_accessed=returned.size * 10, transcendentals=0
        ),
        name="cost_phase",
    )(phase, returned)


def swap(values):
    return lax.all_to_all(values, SWAP_AXES, split_axis=0, concat_axis=0, tiled=True)


def per_device(
    state_real, state_imag, adjoint_real, adjoint_imag, energies, gamma_angle, beta_angle
):
    local_size = state_real.shape[0]
    devices = lax.axis_size(AXES)
    whole_size = local_size * devices
    qubits = whole_size.bit_length() - 1
    shape = (devices, local_size // (devices * LANES), LANES)
    arrays = [
        part.reshape(shape) for part in (state_real, state_imag, adjoint_real, adjoint_imag)
    ]
    there = swap(pre_rotate(beta_angle, *arrays)).reshape(devices, -1, LANES)
    matrix, tangent, phase, found = prepare(
        qubits, beta_angle, gamma_angle, energies.reshape(-1, LANES)
    )
    elsewhere = exchanged_energies(qubits, shape, found)
    slope = local_slope(*arrays)
    middle = mid_rotate(tangent, matrix, slope, elsewhere, there)
    back = swap(middle.reshape(devices, -1, 1, LANES)).reshape(middle.shape)
    *outputs, gamma_gradient, beta_gradient = last_phase(
        whole_size, phase.reshape((2,) + shape), back
    )
    return tuple(part.reshape(-1) for part in outputs) + (
        gamma_gradient.reshape(1),
        beta_gradient.reshape(1),
    )


def solution(mesh):
    in_specs = (P(AXES),) * 5 + (P(), P())
    out_specs = (P(AXES),) * 4 + (P(), P())
    return jax.shard_map(
        per_device, mesh=mesh, in_specs=in_specs, out_specs=out_specs, check_vma=False
    )
```

```python
import functools

import jax
import jax.numpy as jnp
import numpy as np
from jax import lax
from jax.experimental import pallas as pl
from jax.experimental.pallas import tpu as pltpu
from jax.sharding import PartitionSpec as P

AXES = ("gx", "gy", "gz")
LANES = 128
SUB = 8
VMEM_BYTES = 12 * 1024 * 1024
MID_VMEM_BYTES = 24 * 1024 * 1024
LARGE_VMEM_BYTES = 60 * 1024 * 1024


def sin_cos(angle):
    turns = jnp.round(angle * 0.6366197723675814)
    rest = angle - turns * 1.5703125
    rest = rest - turns * 4.837512969970703125e-4
    rest = rest - turns * 7.54978995489188216e-8
    square = rest * rest
    sine = (-1.9515295891e-4 * square + 8.3321608736e-3) * square - 1.6666654611e-1
    sine = rest + rest * square * sine
    cosine = (2.443315711809948e-5 * square - 1.388731625493765e-3) * square
    cosine = 1.0 - 0.5 * square + square * square * (cosine + 4.166664568298827e-2)
    quadrant = turns.astype(jnp.int32) & 3
    swap = (quadrant & 1) == 1
    sine, cosine = jnp.where(swap, cosine, sine), jnp.where(swap, sine, cosine)
    sine = jnp.where(quadrant >= 2, -sine, sine)
    cosine = jnp.where((quadrant == 1) | (quadrant == 2), -cosine, cosine)
    return sine, cosine


def splat(number_ref):
    return jnp.full((SUB, LANES), number_ref[0], jnp.float32)


def split_in_two(values):
    high = values.astype(jnp.bfloat16)
    return high, (values - high.astype(jnp.float32)).astype(jnp.bfloat16)


def flip_sublane(tiles, bit):
    if 2 * bit == SUB:
        return pltpu.roll(tiles, bit, 1)
    row = lax.broadcasted_iota(jnp.int32, tiles.shape, 1)
    return jnp.where(
        (row & bit) == 0, pltpu.roll(tiles, SUB - bit, 1), pltpu.roll(tiles, bit, 1)
    )


def rotate_bits(items, tangent):
    bit = 1
    while bit < len(items):
        items = [
            (
                items[pos][0] - tangent * items[pos ^ bit][1],
                items[pos][1] + tangent * items[pos ^ bit][0],
            )
            for pos in range(len(items))
        ]
        bit *= 2
    return items


def rotate_leading(load, store, count, tangent, group_bits=3):
    finished = 0
    total = count.bit_length() - 1
    while finished < total:
        width = min(group_bits, total - finished)
        stride = 1 << finished
        size = 1 << width
        for base in range(count):
            if base & (stride * (size - 1)):
                continue
            items = [load(base + stride * pos, finished > 0) for pos in range(size)]
            items = rotate_bits(items, tangent)
            for pos in range(size):
                store(base + stride * pos, items[pos])
        finished += width


def pre_kernel(
    beta_ref, sr_ref, si_ref, ar_ref, ai_ref, out_ref, held, turned, in_sem, out_sem
):
    count, rows, _ = sr_ref.shape
    tiles = rows // SUB
    sources = (sr_ref, si_ref, ar_ref, ai_ref)

    def fetch(tile, part):
        return pltpu.make_async_copy(
            sources[part].at[:, pl.ds(tile * SUB, SUB), :],
            held.at[tile, part],
            in_sem.at[tile, part],
        )

    def write(tile, pair):
        return pltpu.make_async_copy(
            turned.at[tile, pair],
            out_ref.at[:, pl.ds(2 * pair, 2), pl.ds(tile * SUB, SUB), :],
            out_sem.at[tile, pair],
        )

    for tile in range(tiles):
        for part in range(4):
            fetch(tile, part).start()
    sine, cosine = sin_cos(splat(beta_ref))
    tangent = sine / cosine
    for tile in range(tiles):
        for pair in range(2):
            for part in range(2):
                fetch(tile, 2 * pair + part).wait()

            def load(pos, again):
                if again:
                    return turned[tile, pair, pos, 0], turned[tile, pair, pos, 1]
                return held[tile, 2 * pair, pos], held[tile, 2 * pair + 1, pos]

            def store(pos, item):
                turned[tile, pair, pos, 0] = item[0]
                turned[tile, pair, pos, 1] = item[1]

            rotate_leading(load, store, count, tangent)
            write(tile, pair).start()
    for tile in range(tiles):
        for pair in range(2):
            write(tile, pair).wait()


def pre_rotate(beta, sr, si, ar, ai):
    count, rows, _ = sr.shape
    tiles = rows // SUB
    hbm = pl.BlockSpec(memory_space=pltpu.HBM)
    size = count * rows * LANES
    return pl.pallas_call(
        pre_kernel,
        in_specs=[pl.BlockSpec(memory_space=pltpu.SMEM)] + [hbm] * 4,
        out_specs=hbm,
        out_shape=jax.ShapeDtypeStruct((count, 4, rows, LANES), jnp.float32),
        scratch_shapes=[
            pltpu.VMEM((tiles, 4, count, SUB, LANES), jnp.float32),
            pltpu.VMEM((tiles, 2, count, 2, SUB, LANES), jnp.float32),
            pltpu.SemaphoreType.DMA((tiles, 4)),
            pltpu.SemaphoreType.DMA((tiles, 2)),
        ],
        compiler_params=pltpu.CompilerParams(vmem_limit_bytes=LARGE_VMEM_BYTES),
        cost_estimate=pl.CostEstimate(
            flops=size * 40, bytes_accessed=size * 32, transcendentals=0
        ),
        name="rotate_top",
    )(beta, sr, si, ar, ai)


def prep_kernel(
    qubits, beta_ref, energy_ref, matrix_ref, tangent_ref, found_ref
):
    sine, cosine = sin_cos(splat(beta_ref))
    tangent_ref[...] = sine / cosine
    sine, cosine = sine[:1], cosine[:1]
    scale = jnp.ones_like(cosine)
    for _ in range(qubits - 7):
        scale = scale * cosine
    powers = []
    for ones in range(8):
        value = scale
        for _ in range(7 - ones):
            value = value * cosine
        for _ in range(ones):
            value = value * sine
        powers.append(-value if ones & 2 else value)
    row = lax.broadcasted_iota(jnp.int32, (LANES, LANES), 0)
    column = lax.broadcasted_iota(jnp.int32, (LANES, LANES), 1)
    ones = lax.population_count(row ^ column)
    real_part = jnp.zeros((LANES, LANES), jnp.float32)
    imag_part = jnp.zeros((LANES, LANES), jnp.float32)
    for number in range(8):
        if number & 1:
            imag_part = jnp.where(ones == number, powers[number], imag_part)
        else:
            real_part = jnp.where(ones == number, powers[number], real_part)
    real_high, real_low = split_in_two(real_part)
    imag_high, imag_low = split_in_two(imag_part)
    for place, real_term, imag_term in (
        (0, real_high, imag_high),
        (1, real_high, imag_high),
        (2, real_low, imag_low),
    ):
        upper = pl.ds(2 * LANES * place, LANES)
        lower = pl.ds(2 * LANES * place + LANES, LANES)
        matrix_ref[upper, :LANES] = real_term
        matrix_ref[upper, LANES:] = imag_term
        matrix_ref[lower, :LANES] = -imag_term
        matrix_ref[lower, LANES:] = real_term

    local_size = energy_ref.shape[0] * LANES
    tiles = 4 * SUB

    def step(pos, best):
        rows = pl.ds(pl.multiple_of(pos * tiles, tiles), tiles)
        energy = energy_ref[rows, :]
        index = (
            lax.broadcasted_iota(jnp.int32, energy.shape, 0) * LANES
            + lax.broadcasted_iota(jnp.int32, energy.shape, 1)
            + pos * (tiles * LANES)
        )
        return jnp.maximum(best, energy * local_size + index)

    best = lax.fori_loop(
        0, energy_ref.shape[0] // tiles, step, jnp.zeros((tiles, LANES), jnp.int32)
    )
    found_ref[...] = jnp.max(best.reshape(-1, SUB, LANES), axis=0)


def prepare(qubits, beta, energies):
    rows = energies.shape[0]
    smem = pl.BlockSpec(memory_space=pltpu.SMEM)
    vmem = pl.BlockSpec(memory_space=pltpu.VMEM)
    return pl.pallas_call(
        functools.partial(prep_kernel, qubits),
        in_specs=[smem, vmem],
        out_specs=[vmem] * 3,
        out_shape=[
            jax.ShapeDtypeStruct((6 * LANES, 2 * LANES), jnp.bfloat16),
            jax.ShapeDtypeStruct((SUB, LANES), jnp.float32),
            jax.ShapeDtypeStruct((SUB, LANES), jnp.int32),
        ],
        compiler_params=pltpu.CompilerParams(vmem_limit_bytes=VMEM_BYTES),
        cost_estimate=pl.CostEstimate(
            flops=rows * LANES * 4, bytes_accessed=rows * LANES * 4, transcendentals=0
        ),
        name="lane_matrix",
    )(beta, energies)


def phase_kernel(token_ref, gamma_ref, energy_ref, phase_ref):
    gamma = gamma_ref[0]
    tiles = 4 * SUB

    def step(pos, carry):
        rows = pl.ds(pl.multiple_of(pos * tiles, tiles), tiles)
        sine, cosine = sin_cos(gamma * energy_ref[rows, :].astype(jnp.float32))
        phase_ref[0, rows, :] = cosine
        phase_ref[1, rows, :] = sine
        return carry

    lax.fori_loop(0, energy_ref.shape[0] // tiles, step, 0)


def cost_phases(token, gamma, energies):
    rows = energies.shape[0]
    smem = pl.BlockSpec(memory_space=pltpu.SMEM)
    vmem = pl.BlockSpec(memory_space=pltpu.VMEM)
    return pl.pallas_call(
        phase_kernel,
        in_specs=[vmem, smem, vmem],
        out_specs=vmem,
        out_shape=jax.ShapeDtypeStruct((2, rows, LANES), jnp.float32),
        compiler_params=pltpu.CompilerParams(vmem_limit_bytes=VMEM_BYTES),
        cost_estimate=pl.CostEstimate(
            flops=rows * LANES * 50, bytes_accessed=rows * LANES * 12, transcendentals=0
        ),
        name="phases",
    )(token, gamma, energies)


def labs_energy(spins, qubits, count_ones):
    energy = 0
    for lag in range(1, qubits):
        span = qubits - lag
        differ = count_ones((spins ^ (spins >> lag)) & ((1 << span) - 1))
        correlation = span - 2 * differ
        energy = energy + correlation * correlation
    return energy


@functools.lru_cache(maxsize=None)
def highest_table(qubits, local_bits):
    every = 2**qubits - 1
    second = sum(2**place for place in range(0, qubits, 2))
    same = [value >> local_bits for value in (0, every, second, every ^ second)]
    low = np.arange(2**local_bits, dtype=np.int32)
    table, covered = {}, set()
    for top in range(2 ** (qubits - local_bits)):
        if top in covered:
            continue
        covered.update(top ^ value for value in same)
        energy = labs_energy(
            low | np.int32(top << local_bits),
            qubits,
            lambda bits: np.bitwise_count(bits).astype(np.int32),
        )
        highest = int(energy.max())
        places = np.flatnonzero(energy == highest)
        if highest in table or len(places) > 1:
            return None
        table[highest] = (top << local_bits) | int(places[0])
    return table


def energy_kernel(qubits, table, found_ref, token_ref, out_ref):
    count, rows, _ = out_ref.shape
    block = rows * LANES
    local_bits = (count * block).bit_length() - 1
    found = found_ref[...]
    device = lax.axis_index(AXES)
    if table is None:
        mask = found
    else:
        for shift in (1, 2, 4):
            found = jnp.maximum(found, pltpu.roll(found, shift, 0))
        for shift in (1, 2, 4, 8, 16, 32, 64):
            found = jnp.maximum(found, pltpu.roll(found, shift, 1))
        highest = found >> local_bits
        mask = (found & ((1 << local_bits) - 1)) + (device << local_bits)
        for value, index in table.items():
            mask = jnp.where(highest == value, mask ^ index, mask)
    offset = (
        lax.broadcasted_iota(jnp.int32, (SUB, LANES), 0) * LANES
        + lax.broadcasted_iota(jnp.int32, (SUB, LANES), 1)
    ) ^ mask
    tiles = rows // SUB

    def step(pos, carry):
        for tile in range(tiles):
            place = (pos << local_bits) + device * block + tile * (SUB * LANES)
            spins = offset ^ place
            energy = jnp.zeros((SUB, LANES), jnp.float32)
            for lag in range(1, qubits):
                span = qubits - lag
                differ = lax.population_count((spins ^ (spins >> lag)) & ((1 << span) - 1))
                correlation = (span - 2 * differ).astype(jnp.float32)
                energy = energy + correlation * correlation
            out_ref[pos, pl.ds(tile * SUB, SUB), :] = energy
        return carry

    lax.fori_loop(0, count, step, 0)


def exchanged_energies(qubits, shape, found, token):
    local_bits = (shape[0] * shape[1] * shape[2]).bit_length() - 1
    table = highest_table(qubits, local_bits)
    if table is None:
        highest = sum(span * span for span in range(1, qubits))
        index = (found & ((1 << local_bits) - 1)) + (lax.axis_index(AXES) << local_bits)
        index = jnp.max(jnp.where(found >> local_bits == highest, index, -1))
        found = jnp.full((SUB, LANES), lax.pmax(index, AXES), jnp.int32)
    vmem = pl.BlockSpec(memory_space=pltpu.VMEM)
    return pl.pallas_call(
        functools.partial(energy_kernel, qubits, table),
        in_specs=[vmem, vmem],
        out_specs=vmem,
        out_shape=jax.ShapeDtypeStruct(shape, jnp.float32),
        compiler_params=pltpu.CompilerParams(vmem_limit_bytes=VMEM_BYTES),
        cost_estimate=pl.CostEstimate(
            flops=(200 << local_bits), bytes_accessed=(4 << local_bits), transcendentals=0
        ),
        name="energies",
    )(found, token)


def tile_place(place, number, tiles):
    first = (place * (tiles * SUB + 1) + SUB - 1) // SUB
    if number == tiles - 1 and place % SUB not in (0, SUB - 1):
        return None, (first - 1, first + tiles - 1)
    return first + number, None


def shared_tile(place, tiles):
    return ((place + 1) * (tiles * SUB + 1) - 1) // SUB


def mid_kernel(
    tangent_ref,
    matrix_ref,
    slope_ref,
    energy_ref,
    in_ref,
    out_ref,
    token_ref,
    energies,
    split,
    wide,
    edge,
    energy_sem,
):
    count, rows, _ = energy_ref.shape
    tiles = rows // SUB
    fetch = pltpu.make_async_copy(energy_ref, energies, energy_sem)
    fetch.start()
    tangent = tangent_ref[...]
    token_ref[...] = tangent
    span = max(1, 64 // rows)

    def rotate_rows(pos, pair_pos):
        some = pl.ds(pos * span, span)
        there = pl.ds(pl.multiple_of(pos * (span * rows), span * rows), span * rows)
        pair = [
            in_ref[some, pl.ds((2 * pair_pos + part) * rows, rows), :].reshape(
                span, tiles, SUB, LANES
            )
            for part in range(2)
        ]
        bit = 1
        while bit < tiles:
            other = [
                jnp.concatenate(
                    [part[:, tile ^ bit : (tile ^ bit) + 1] for tile in range(tiles)], axis=1
                )
                for part in pair
            ]
            pair = [pair[0] - tangent * other[1], pair[1] + tangent * other[0]]
            bit *= 2
        pair = [part.reshape(span * tiles, SUB, LANES) for part in pair]
        for bit in (1, 2, 4):
            other = [flip_sublane(part, bit) for part in pair]
            pair = [pair[0] - tangent * other[1], pair[1] + tangent * other[0]]
        for part in range(2):
            first, second = split_in_two(pair[part].reshape(span * rows, LANES))
            for place, term in ((0, first), (1, second), (2, first)):
                start = (2 * place + part) * LANES
                split[pair_pos, there, start : start + LANES] = term

    def rotate_lanes(pair_pos, pos):
        there = pl.ds(pos * half, half)
        wide[pair_pos, there, :] = jnp.dot(
            split[pair_pos, there, :], matrix_ref[...], preferred_element_type=jnp.float32
        )

    half = count * rows // 2
    steps = count // span

    def two_steps(pos, carry):
        for more in range(2):
            rotate_rows(2 * pos + more, 0)
        return carry

    lax.fori_loop(0, steps // 2, two_steps, 0)
    for pos in range(2):
        rotate_lanes(0, pos)
        for step in range(pos * steps // 2, (pos + 1) * steps // 2):
            rotate_rows(step, 1)
    for pos in range(2):
        rotate_lanes(1, pos)
    fetch.wait()

    def group(tile, bits, places):
        pairs = []
        for pair_pos in range(2):
            items = []
            for place in places:
                here = pl.ds(place * rows + tile * SUB, SUB)
                items.append([wide[pair_pos, here, :LANES], wide[pair_pos, here, LANES:]])
            pairs.append(rotate_bits(items, tangent))
        state, adjoint = pairs
        share = 0.0
        for pos in range(len(places)):
            flipped = [
                functools.reduce(
                    jnp.add, [state[pos ^ (1 << bit)][part] for bit in range(bits)]
                )
                for part in range(2)
            ]
            share = share + (adjoint[pos][0] * flipped[1] - adjoint[pos][1] * flipped[0])
        return pairs, share

    beta_sum = slope_ref[...]
    gamma_sum = jnp.zeros((SUB, LANES), jnp.float32)
    total_bits = count.bit_length() - 1
    last_bits = min(3, total_bits)
    finished, left = last_bits, total_bits
    while finished < total_bits:
        bits = min(3, total_bits - finished)
        left -= bits
        stride = 1 << finished
        total = jnp.zeros((SUB, LANES), jnp.float32)
        for tile in range(tiles):
            for base in range(count):
                if base & (stride * ((1 << bits) - 1)):
                    continue
                places = [base + stride * pos for pos in range(1 << bits)]
                pairs, share = group(tile, bits, places)
                total = total + share
                for pair_pos, items in enumerate(pairs):
                    for place, item in zip(places, items):
                        here = pl.ds(place * rows + tile * SUB, SUB)
                        wide[pair_pos, here, :LANES] = item[0]
                        wide[pair_pos, here, LANES:] = item[1]
        for _ in range(left):
            total = total * (1.0 + tangent * tangent)
        beta_sum = beta_sum + total
        finished += bits

    block_tiles = 4 * tiles
    for base in range(0, count, 1 << last_bits):
        places = range(base, base + (1 << last_bits))
        for tile in range(tiles):
            pairs, share = group(tile, last_bits, places)
            state, adjoint = pairs
            beta_sum = beta_sum + share
            for pos, place in enumerate(places):
                value = adjoint[pos][0] * state[pos][1] - adjoint[pos][1] * state[pos][0]
                energy = energies[place, pl.ds(tile * SUB, SUB), :]
                gamma_sum = gamma_sum + energy * value
                for part in range(4):
                    item = pairs[part // 2][pos][part % 2]
                    whole, halves = tile_place(place, part * tiles + tile, block_tiles)
                    if halves:
                        edge[place] = item
                    else:
                        out_ref[pl.ds(whole * SUB, SUB), :] = item

    beta_row = jnp.sum(beta_sum, axis=0, keepdims=True)
    gamma_row = jnp.sum(gamma_sum, axis=0, keepdims=True)
    half_lanes = LANES // 2
    lane = lax.broadcasted_iota(jnp.int32, (1, LANES), 1)
    value = jnp.where(
        lane < half_lanes,
        beta_row + pltpu.roll(beta_row, half_lanes, 1),
        gamma_row + pltpu.roll(gamma_row, half_lanes, 1),
    )
    value = jnp.broadcast_to(value, (SUB, LANES))
    row = lax.broadcasted_iota(jnp.int32, (SUB, LANES), 0)
    for place in range(count):
        sublane = place % SUB
        if sublane == SUB - 1:
            continue
        tile = value
        if 0 < sublane:
            tile = jnp.where(row < sublane, edge[place], tile)
        if sublane < SUB - 2:
            tile = jnp.where(row > sublane, edge[place + 1], tile)
        out_ref[pl.ds(shared_tile(place, block_tiles) * SUB, SUB), :] = tile


def mid_rotate(tangent, matrix, slope, energies, received):
    count, rows, _ = energies.shape
    size = received.size
    flat = (2, count * rows)
    out_shape = (count * (4 * rows + 1), LANES)
    vmem = pl.BlockSpec(memory_space=pltpu.VMEM)
    return pl.pallas_call(
        mid_kernel,
        in_specs=[vmem, vmem, vmem, pl.BlockSpec(memory_space=pltpu.HBM), vmem],
        out_specs=[vmem, vmem],
        out_shape=[
            jax.ShapeDtypeStruct(out_shape, jnp.float32),
            jax.ShapeDtypeStruct((SUB, LANES), jnp.float32),
        ],
        scratch_shapes=[
            pltpu.VMEM(energies.shape, jnp.float32),
            pltpu.VMEM(flat + (6 * LANES,), jnp.bfloat16),
            pltpu.VMEM(flat + (2 * LANES,), jnp.float32),
            pltpu.VMEM((count, SUB, LANES), jnp.float32),
            pltpu.SemaphoreType.DMA,
        ],
        compiler_params=pltpu.CompilerParams(vmem_limit_bytes=MID_VMEM_BYTES),
        cost_estimate=pl.CostEstimate(
            flops=size * 2 * 256 * 3, bytes_accessed=size * 8, transcendentals=0
        ),
        name="rotate_rest",
    )(tangent, matrix, slope, energies, received)


def slope_kernel(sr_ref, si_ref, ar_ref, ai_ref, out_ref):
    count, rows, _ = sr_ref.shape
    tiles = rows // SUB
    row = lax.broadcasted_iota(jnp.int32, (LANES, LANES), 0)
    column = lax.broadcasted_iota(jnp.int32, (LANES, LANES), 1)
    flips = (lax.population_count(row ^ column) == 1).astype(jnp.float32)

    def step(pos, total):
        def flipped(ref):
            own = ref[pos]
            near = own.reshape(tiles, SUB, LANES)
            result = jnp.dot(
                own,
                flips,
                precision=lax.Precision.HIGHEST,
                preferred_element_type=jnp.float32,
            ).reshape(tiles, SUB, LANES)
            for bit in (1, 2, 4):
                result = result + flip_sublane(near, bit)
            bit = 1
            while bit < tiles:
                result = result + jnp.concatenate(
                    [near[tile ^ bit : (tile ^ bit) + 1] for tile in range(tiles)], axis=0
                )
                bit *= 2
            bit = 1
            while bit < count:
                result = result + ref[pos ^ bit].reshape(tiles, SUB, LANES)
                bit *= 2
            return result

        real_part, imag_part = flipped(sr_ref), flipped(si_ref)
        adjoint_real = ar_ref[pos].reshape(tiles, SUB, LANES)
        adjoint_imag = ai_ref[pos].reshape(tiles, SUB, LANES)
        part = adjoint_real * imag_part - adjoint_imag * real_part
        return total + jnp.sum(part, axis=0)

    out_ref[...] = lax.fori_loop(0, count, step, jnp.zeros((SUB, LANES), jnp.float32))


def local_slope(sr, si, ar, ai):
    vmem = pl.BlockSpec(memory_space=pltpu.VMEM)
    return pl.pallas_call(
        slope_kernel,
        in_specs=[vmem] * 4,
        out_specs=vmem,
        out_shape=jax.ShapeDtypeStruct((SUB, LANES), jnp.float32),
        compiler_params=pltpu.CompilerParams(vmem_limit_bytes=VMEM_BYTES),
        cost_estimate=pl.CostEstimate(
            flops=sr.size * 2 * 2 * LANES * 6, bytes_accessed=sr.size * 16, transcendentals=0
        ),
        name="local_slope",
    )(sr, si, ar, ai)


def last_kernel(whole_size, phase_ref, in_ref, *refs):
    out_refs, (gamma_ref, beta_ref, done, out_sem) = refs[:4], refs[4:]
    _, count, rows, _ = phase_ref.shape
    parts = out_sem.shape[0]
    bounds = [count * place // 16 for place in (0, 2, 7, 13, 16)]
    tiles = rows // SUB
    row = lax.broadcasted_iota(jnp.int32, (SUB, LANES), 0)

    def write(pos, place):
        some = pl.ds(bounds[pos], bounds[pos + 1] - bounds[pos])
        return pltpu.make_async_copy(
            done.at[place, some], out_refs[place].at[some], out_sem.at[pos, place]
        )

    sublane = lax.axis_index(AXES) & (SUB - 1)
    skip = (SUB - sublane) & (SUB - 1)
    below = jnp.where(sublane == SUB - 1, SUB, sublane)
    block_tiles = 4 * tiles
    block = block_tiles * SUB + 1

    def load(pos, number):
        start = pos * block
        if number < block_tiles - 1:
            return in_ref[pl.ds(start + skip + number * SUB, SUB), :]
        first = pltpu.roll(in_ref[pl.ds(start, SUB), :], sublane, 0)
        last = in_ref[pl.ds(start + block - SUB, SUB), :]
        last = pltpu.roll(last, (sublane + 1) & (SUB - 1), 0)
        whole = in_ref[pl.ds(start + block - 1 - SUB, SUB), :]
        return jnp.where(sublane == 0, whole, jnp.where(row < below, last, first))

    for part in range(parts):
        for pos in range(bounds[part], bounds[part + 1]):
            for tile in range(tiles):
                here = pl.ds(tile * SUB, SUB)
                cosine, sine = phase_ref[0, pos, here], phase_ref[1, pos, here]
                sr, si, ar, ai = (load(pos, place * tiles + tile) for place in range(4))
                done[0, pos, here] = sr * cosine - si * sine
                done[1, pos, here] = sr * sine + si * cosine
                done[2, pos, here] = ar * cosine - ai * sine
                done[3, pos, here] = ar * sine + ai * cosine
        for place in range(4):
            write(part, place).start()
    extra = jnp.where(sublane == SUB - 1, 0, block - 1)
    total = in_ref[pl.ds(extra, 1), :]
    for pos in range(1, count):
        total = total + in_ref[pl.ds(pos * block + extra, 1), :]
    first = lax.broadcasted_iota(jnp.int32, (1, LANES), 1) < LANES // 2
    beta_ref[...] = jnp.sum(jnp.where(first, total, 0.0), axis=1, keepdims=True) / whole_size
    gamma_ref[...] = jnp.sum(jnp.where(first, 0.0, total), axis=1, keepdims=True) / whole_size
    for part in range(parts):
        for place in range(4):
            write(part, place).wait()


def last_phase(whole_size, phase, returned):
    _, count, rows, _ = phase.shape
    parts = 4
    shape = jax.ShapeDtypeStruct((count, rows, LANES), jnp.float32)
    number = jax.ShapeDtypeStruct((1, 1), jnp.float32)
    vmem = pl.BlockSpec(memory_space=pltpu.VMEM)
    hbm = pl.BlockSpec(memory_space=pltpu.HBM)
    return pl.pallas_call(
        functools.partial(last_kernel, whole_size),
        in_specs=[vmem] * 2,
        out_specs=[hbm] * 4 + [vmem] * 2,
        out_shape=[shape] * 4 + [number] * 2,
        scratch_shapes=[
            pltpu.VMEM((4, count, rows, LANES), jnp.float32),
            pltpu.SemaphoreType.DMA((parts, 4)),
        ],
        compiler_params=pltpu.CompilerParams(vmem_limit_bytes=VMEM_BYTES),
        cost_estimate=pl.CostEstimate(
            flops=returned.size * 3, bytes_accessed=returned.size * 10, transcendentals=0
        ),
        name="cost_phase",
    )(phase, returned)


def swap(values):
    return lax.all_to_all(values, AXES, split_axis=0, concat_axis=0, tiled=True)


def per_device(
    state_real, state_imag, adjoint_real, adjoint_imag, energies, gamma_angle, beta_angle
):
    local_size = state_real.shape[0]
    devices = lax.axis_size(AXES)
    whole_size = local_size * devices
    qubits = whole_size.bit_length() - 1
    shape = (devices, local_size // (devices * LANES), LANES)
    arrays = [
        part.reshape(shape) for part in (state_real, state_imag, adjoint_real, adjoint_imag)
    ]
    there = swap(pre_rotate(beta_angle, *arrays)).reshape(devices, -1, LANES)
    energies = energies.reshape(-1, LANES)
    matrix, tangent, found = prepare(qubits, beta_angle, energies)
    slope = local_slope(*arrays)
    elsewhere = exchanged_energies(qubits, shape, found, slope)
    middle, token = mid_rotate(tangent, matrix, slope, elsewhere, there)
    back = swap(middle.reshape(devices, -1, 1, LANES)).reshape(middle.shape)
    phase = cost_phases(token, gamma_angle, energies)
    *outputs, gamma_gradient, beta_gradient = last_phase(
        whole_size, phase.reshape((2,) + shape), back
    )
    return tuple(part.reshape(-1) for part in outputs) + (
        gamma_gradient.reshape(1),
        beta_gradient.reshape(1),
    )


def solution(mesh):
    in_specs = (P(AXES),) * 5 + (P(), P())
    out_specs = (P(AXES),) * 4 + (P(), P())
    return jax.shard_map(
        per_device, mesh=mesh, in_specs=in_specs, out_specs=out_specs, check_vma=False
    )
```
